32 devices in a mesh: ctx: 8 (over z, x), head: 4 (over y, core).
Axes of the slice: x: 2, y: 2, z: 4, core: 2. Of those that a mesh axis runs over, the one named last changes fastest.
Arguments:
- queries: bfloat16 [4096, 2048], P('ctx', 'head'), may hold values from -6 to 6
- key_rows: bfloat16 [4096, 2048], P('ctx', 'head'), may hold values from -6 to 6
- value_rows: bfloat16 [4096, 2048], P('ctx', 'head'), may hold values from -6 to 6
- targets: bfloat16 [4096, 512], P('ctx'), may hold values from -2.5 to 2.5
- readout: bfloat16 [512, 4096], P(None, 'head'), may hold values from -0.25 to 0.25
- retain: float32 [8, 16], P('ctx', 'head'), may hold values from 0.3 to 1
- learn_rate: float32 [8, 16], P('ctx', 'head'), may hold values from 0.01 to 0.1
- allowed: int32 [8, 2], replicated, may hold values 0 or 1
- positions: int32 [8, 128], P('ctx'), may hold values from 0 to 511, as said below
- grad_out: bfloat16 [4096, 2048], P('ctx', 'head'), may hold values from -6 to 6
Outputs:
- grad_queries: float32 [4096, 2048], P('ctx', 'head')
- grad_keys: float32 [4096, 2048], P('ctx', 'head')
- grad_values: float32 [4096, 2048], P('ctx', 'head')
- grad_targets: float32 [4096, 512], P('ctx', 'head')
- grad_readout: float32 [512, 4096], P('ctx', 'head')
The draws below stay inside these ranges and needn't reach their ends.
Inputs may be any that keep to these rules, and one draw needn't show every extreme that they name: The 128 positions of a segment are distinct, ascending, and include 0 and 511.
All inputs are finite; a program needn't handle non-finite values.
Results may differ from the reference program's by a relative error of at most 0.0081.
Values may be sent and summed in bfloat16 or wider, within the bound.
No kernel may reach another device: no remote copies, remote signals or barrier semaphores. Data moves between devices by JAX's collectives and lax.ppermute only.
A program may use at most 192 MiB of HBM per device.

```python
import math
import jax
import jax.numpy as jnp
from jax import lax

HEAD_COUNT = 16
DK = 128
FH = 512
SEG = 512
NM = 128
W = 2
D = 2048
SEGMENT_TOTAL = 8
TOKENS = 4096


def draw_retain(key, part):
    key_collection = jax.random.split(jax.random.fold_in(key, 31), 5)
    fast_count = HEAD_COUNT // 2
    head_order = jax.random.permutation(key_collection[0], HEAD_COUNT)
    slow_heads = (head_order >= fast_count)[None, :]
    spread = jax.random.uniform(key_collection[1], (SEGMENT_TOTAL, HEAD_COUNT), minval=0.3, maxval=1.5)
    gentle_learning_rate = jnp.exp(-spread / SEGMENT_TOTAL)
    fast_rate = jax.random.uniform(key_collection[2], (SEGMENT_TOTAL, HEAD_COUNT), minval=0.45, maxval=0.6)
    spike_row_count = jax.random.uniform(key_collection[3], (SEGMENT_TOTAL, 1)) < 3.0 / SEGMENT_TOTAL
    spike_multiplier = jax.random.uniform(key_collection[4], (SEGMENT_TOTAL, HEAD_COUNT), minval=0.5, maxval=0.8)
    gentle_value = gentle_learning_rate * jnp.where(spike_row_count, spike_multiplier, 1.0)
    return jnp.where(slow_heads, gentle_value, fast_rate).astype(jnp.float32)


def draw_positions(key, part):
    row_keys = jax.random.split(jax.random.fold_in(key, 17), SEGMENT_TOTAL)
    inner_rows = jax.vmap(lambda row_key: jax.random.permutation(row_key, SEG - 2))(row_keys)[:, :NM - 2] + 1
    first_column = jnp.zeros((SEGMENT_TOTAL, 1), jnp.int32)
    last_column = jnp.full((SEGMENT_TOTAL, 1), SEG - 1, jnp.int32)
    return jnp.sort(jnp.concatenate([first_column, inner_rows.astype(jnp.int32), last_column], axis=1), axis=1)


def drawn_rows(key, salt):
    return jnp.clip(jax.random.normal(jax.random.fold_in(key, salt), (TOKENS, D), jnp.float32), -6.0, 6.0)


def draw_queries(key, part):
    filled = drawn_rows(key, 1)
    return filled.astype(jnp.bfloat16)


def draw_key_rows(key, part):
    filled = drawn_rows(key, 2)
    return filled.astype(jnp.bfloat16)


def touch_ends(drawn, own_key, smallest, largest):
    longest = drawn.shape.index(max(drawn.shape))
    spots = []
    for shift in (0, 1):
        where = [jax.random.randint(jax.random.fold_in(own_key, axis), (), 0, length) for axis, length in enumerate(drawn.shape)]
        where[longest] = (where[longest] + shift) % drawn.shape[longest]
        spots.append(tuple(where))
    return drawn.at[spots[0]].set(smallest).at[spots[1]].set(largest)


def shard_levels(rng, shape, cuts, low, largest):
    gain, own = 1.0, jax.random.fold_in(rng, 6)
    for axis_at, shards_of in cuts:
        draws = jnp.exp(jax.random.uniform(jax.random.fold_in(own, axis_at), (shards_of,), jnp.float32, low / len(cuts), largest / len(cuts)))
        gain = gain * jnp.repeat(draws, shape[axis_at] // shards_of).reshape([-1 if axis == axis_at else 1 for axis in range(len(shape))])
    return gain


def normal_values(rng, extent, scale, reach, shards=(), kind=jnp.bfloat16):
    result = jax.random.normal(rng, extent, jnp.float32) * scale
    if len(shards) > 0:
        result = shard_levels(rng, extent, shards, -0.22, 0.18) * result
    return jnp.clip(result, min=-reach, max=reach).astype(kind)


def setup_inputs(seed: int = 0) -> dict:
    streams_of = jax.random.split(jax.random.key(seed), 11)
    return {
        "queries": draw_queries(jax.random.fold_in(streams_of[10], 71), 0),
        "key_rows": draw_key_rows(jax.random.fold_in(streams_of[10], 71), 0),
        "value_rows": normal_values(streams_of[2], (TOKENS, D), 1.0, 6.0, ((0, 8), (1, 4))),
        "targets": normal_values(streams_of[3], (TOKENS, FH), 0.3, 2.5, ((0, 8),)),
        "readout": normal_values(streams_of[4], (FH, 2 * D), FH ** -0.5, 0.25, ((1, 4),)),
        "retain": draw_retain(jax.random.fold_in(streams_of[10], 71), 0),
        "learn_rate": jnp.clip(jnp.exp(math.log(0.1) - 2.3025851 * jax.random.uniform(streams_of[6], (SEGMENT_TOTAL, HEAD_COUNT), jnp.float32) ** shard_levels(streams_of[6], (SEGMENT_TOTAL, HEAD_COUNT), ((0, 8), (1, 4)), -0.2, 0.2)), 0.01, 0.1),
        "allowed": touch_ends((jax.random.randint(streams_of[7], (SEGMENT_TOTAL, W), 0, 3) < 2).astype(jnp.int32), jax.random.fold_in(streams_of[7], 1), 0, 1),
        "positions": draw_positions(jax.random.fold_in(streams_of[10], 71), 0),
        "grad_out": normal_values(streams_of[9], (TOKENS, D), 1.0, 6.0, ((0, 8), (1, 4))),
    }


masked_score = -1.0e30
highest = lax.Precision.HIGHEST


def low_copy(values):
    return lax.optimization_barrier(values.astype(jnp.bfloat16)).astype(jnp.float32)


def reference(queries, key_rows, value_rows, targets, readout, retain, learn_rate, allowed, positions, grad_out):
    score_scale = DK ** -0.5
    query_segs = queries.reshape(SEGMENT_TOTAL, SEG, HEAD_COUNT, DK)
    key_segs = key_rows.reshape(SEGMENT_TOTAL, SEG, HEAD_COUNT, DK)
    value_segs = value_rows.reshape(SEGMENT_TOTAL, SEG, HEAD_COUNT, DK)
    cotangent_segs = grad_out.reshape(SEGMENT_TOTAL, SEG, HEAD_COUNT, DK)
    identity_block = jnp.eye(DK, dtype=jnp.float32)
    decay_maps = []
    states = [jnp.zeros((HEAD_COUNT, DK, FH), jnp.float32)]
    for segment in range(SEGMENT_TOTAL):
        keys_wide = key_segs[segment].astype(jnp.float32)
        target_wide = targets[segment * SEG:(segment + 1) * SEG].astype(jnp.float32)
        key_gram = jnp.einsum('sha,shb->hab', keys_wide, keys_wide, precision=highest)
        decay_map = retain[segment][:, None, None] * identity_block - (learn_rate[segment] / SEG)[:, None, None] * key_gram
        write_map = jnp.einsum('sha,sf->haf', keys_wide, target_wide, precision=highest) / SEG
        decay_maps.append(decay_map)
        states.append(jnp.einsum('hab,hbf->haf', decay_map, states[-1], precision=highest) + write_map)
    causal = jnp.arange(SEG)[:, None] >= jnp.arange(SEG)[None, :]
    key_acc = [jnp.zeros((SEG, HEAD_COUNT, DK), jnp.float32) for segment in range(SEGMENT_TOTAL)]
    value_acc = [jnp.zeros((SEG, HEAD_COUNT, DK), jnp.float32) for segment in range(SEGMENT_TOTAL)]
    query_acc = []
    grad_readout = jnp.zeros((FH, 2 * D), jnp.float32)
    grad_states = []
    for segment in range(SEGMENT_TOTAL):
        memory_in = states[segment]
        picked = query_segs[segment][positions[segment]].astype(jnp.float32)
        hidden_read = jnp.einsum('nha,haf->nf', picked, memory_in, precision=highest).astype(jnp.bfloat16)
        memory_tokens = jnp.dot(hidden_read, readout, preferred_element_type=jnp.float32).reshape(NM, HEAD_COUNT, 2, DK)
        key_parts = [memory_tokens[:, :, 0].astype(jnp.bfloat16), key_segs[segment]]
        value_parts = [memory_tokens[:, :, 1].astype(jnp.bfloat16), value_segs[segment]]
        mask_parts = [jnp.ones((SEG, NM), bool), causal]
        for offset in range(1, W + 1):
            source = segment - offset
            if source >= 0:
                key_parts.append(key_segs[source])
                value_parts.append(value_segs[source])
                mask_parts.append(jnp.broadcast_to(allowed[segment, offset - 1] == 1, (SEG, SEG)))
            else:
                key_parts.append(jnp.zeros((SEG, HEAD_COUNT, DK), jnp.bfloat16))
                value_parts.append(jnp.zeros((SEG, HEAD_COUNT, DK), jnp.bfloat16))
                mask_parts.append(jnp.zeros((SEG, SEG), bool))
        keys_all = jnp.concatenate(key_parts, 0).astype(jnp.float32)
        values_all = jnp.concatenate(value_parts, 0).astype(jnp.float32)
        mask_all = jnp.concatenate(mask_parts, 1)
        query_wide = query_segs[segment].astype(jnp.float32)
        cotangent_wide = cotangent_segs[segment].astype(jnp.float32)
        scores = jnp.einsum('ihd,jhd->hij', query_wide, keys_all, precision=highest) * score_scale
        scores = jnp.where(mask_all[None], scores, masked_score)
        exp_scores = jnp.exp(scores - jnp.max(scores, axis=2, keepdims=True))
        probs = exp_scores / jnp.sum(exp_scores, axis=2, keepdims=True)
        probs_low = low_copy(probs)
        attended = jnp.einsum('hij,jhd->hid', probs_low, values_all, precision=highest)
        row_delta = jnp.sum(jnp.transpose(cotangent_wide, (1, 0, 2)) * attended, axis=2, keepdims=True)
        grad_probs = jnp.einsum('ihd,jhd->hij', cotangent_wide, values_all, precision=highest)
        grad_scores = low_copy(probs * (grad_probs - row_delta))
        grad_query = jnp.einsum('hij,jhd->ihd', grad_scores, keys_all, precision=highest) * score_scale
        grad_key = jnp.einsum('hij,ihd->jhd', grad_scores, query_wide, precision=highest) * score_scale
        grad_value = jnp.einsum('hij,ihd->jhd', probs_low, cotangent_wide, precision=highest)
        key_acc[segment] = key_acc[segment] + grad_key[NM:NM + SEG]
        value_acc[segment] = value_acc[segment] + grad_value[NM:NM + SEG]
        for offset in range(1, W + 1):
            source = segment - offset
            if source >= 0:
                lower = NM + offset * SEG
                key_acc[source] = key_acc[source] + grad_key[lower:lower + SEG]
                value_acc[source] = value_acc[source] + grad_value[lower:lower + SEG]
        grad_memory = jnp.stack([grad_key[:NM], grad_value[:NM]], axis=2).reshape(NM, 2 * D).astype(jnp.bfloat16)
        grad_readout = grad_readout + jnp.dot(hidden_read.T, grad_memory, preferred_element_type=jnp.float32)
        grad_hidden = jnp.dot(grad_memory, readout.T, preferred_element_type=jnp.float32)
        grad_picked = jnp.einsum('nf,haf->nha', grad_hidden, memory_in, precision=highest)
        grad_states.append(jnp.einsum('nha,nf->haf', picked, grad_hidden, precision=highest))
        query_acc.append(grad_query.at[positions[segment]].add(grad_picked))
    carried = jnp.zeros((HEAD_COUNT, DK, FH), jnp.float32)
    grad_after = [None] * SEGMENT_TOTAL
    for segment in reversed(range(SEGMENT_TOTAL)):
        grad_after[segment] = carried
        carried = grad_states[segment] + jnp.einsum('hba,hbf->haf', decay_maps[segment], carried, precision=highest)
    target_list = []
    for segment in range(SEGMENT_TOTAL):
        keys_wide = key_segs[segment].astype(jnp.float32)
        target_wide = targets[segment * SEG:(segment + 1) * SEG].astype(jnp.float32)
        later_grad = grad_after[segment]
        grad_decay = jnp.einsum('haf,hbf->hab', later_grad, states[segment], precision=highest)
        symmetric = grad_decay + jnp.swapaxes(grad_decay, 1, 2)
        key_memory = jnp.einsum('sf,haf->sha', target_wide, later_grad, precision=highest) / SEG
        key_memory = key_memory - (learn_rate[segment] / SEG)[None, :, None] * jnp.einsum('sha,hab->shb', keys_wide, symmetric, precision=highest)
        key_acc[segment] = key_acc[segment] + key_memory
        target_list.append(jnp.einsum('sha,haf->sf', keys_wide, later_grad, precision=highest) / SEG)
    grad_queries = jnp.concatenate(query_acc, 0).reshape(TOKENS, D)
    grad_keys = jnp.concatenate(key_acc, 0).reshape(TOKENS, D)
    grad_values = jnp.concatenate(value_acc, 0).reshape(TOKENS, D)
    grad_targets = jnp.concatenate(target_list, 0)
    return grad_queries, grad_keys, grad_values, grad_targets, grad_readout
```

```python
import functools
import math

import jax
import jax.numpy as jnp
from jax import lax
from jax.experimental import pallas as pl
from jax.experimental.pallas import tpu as pltpu
from jax.sharding import PartitionSpec as P

low = jnp.bfloat16
wide = jnp.float32
masked = -1e30
pad_rows = 16
vmem_bytes = 48 * 1024 * 1024

whole_vmem = pl.BlockSpec(memory_space=pltpu.VMEM)
whole_smem = pl.BlockSpec(memory_space=pltpu.SMEM)


def dot(left, right, left_axis=1, right_axis=0):
    return lax.dot_general(
        left, right, (((left_axis,), (right_axis,)), ((), ())), preferred_element_type=wide
    )


def shape_of(shape, dtype):
    return jax.ShapeDtypeStruct(shape, dtype)


def params(grid_rank=0):
    if grid_rank == 0:
        return pltpu.CompilerParams(vmem_limit_bytes=vmem_bytes)
    return pltpu.CompilerParams(
        dimension_semantics=("arbitrary",) * grid_rank, vmem_limit_bytes=vmem_bytes
    )


def cost(flops, moved, exps=0):
    return pl.CostEstimate(flops=int(flops), bytes_accessed=int(moved), transcendentals=int(exps))


def exchange(pieces, axis):
    count = lax.axis_size(axis)
    return [pieces[0]] + [
        lax.ppermute(pieces[bits], axis, [(place, place ^ bits) for place in range(count)])
        for bits in range(1, len(pieces))
    ]


def shifted(value, axis, steps):
    count = lax.axis_size(axis)
    first, last = max(0, -steps), min(count, count - steps)
    return lax.ppermute(value, axis, [(place, place + steps) for place in range(first, last)])


def summed(value, axis):
    count = lax.axis_size(axis)
    bits = 1
    while bits < count:
        sent = value.astype(wide)
        there = lax.ppermute(sent, axis, [(place, place ^ bits) for place in range(count)])
        value = sent.astype(wide) + there.astype(wide)
        bits *= 2
    return value


def pack_kernel(heads, key_ref, target_ref, query_ref, place_ref, retain_ref, rate_ref, *outs):
    pack_refs, picked_ref = outs[:heads], outs[heads]
    seg_len = key_ref.shape[0]
    width = key_ref.shape[1] // heads
    hidden = target_ref.shape[1]
    member = lax.axis_index("ctx") % heads
    for bits in range(heads):
        head = jnp.bitwise_xor(member, bits)
        keys = key_ref[:, pl.ds(pl.multiple_of(head * width, width), width)]
        gram = dot(keys, keys, 0, 0)
        write = dot(keys, target_ref[...], 0, 0)
        out = pack_refs[bits]
        out[:width, :hidden] = (write * (1.0 / seg_len)).astype(low)
        out[:width, hidden:] = (gram * (rate_ref[0, head] * (1.0 / seg_len))).astype(low)
        shape = (pad_rows, hidden + width)
        value = jnp.full(shape, retain_ref[0, head], wide)
        first = value.astype(low).astype(wide)
        second = (value - first).astype(low).astype(wide)
        third = (value - first - second).astype(low).astype(wide)
        row = lax.broadcasted_iota(jnp.int32, shape, 0)
        tail = jnp.where(row == 0, first, jnp.where(row == 1, second, third))
        out[width:, :] = jnp.where(row < 3, tail, 0.0).astype(low)
    rows = lax.broadcasted_iota(jnp.int32, (seg_len, place_ref.shape[1]), 0)
    chosen = jnp.where(rows == place_ref[...], 1.0, 0.0).astype(low)
    picked_ref[...] = dot(chosen, query_ref[...], 0, 0).astype(low)


def pack(key_rows, targets, queries, positions, retain, learn_rate):
    heads = retain.shape[1]
    width = key_rows.shape[1] // heads
    hidden = targets.shape[1]
    packed = shape_of((width + pad_rows, hidden + width), low)
    outs = pl.pallas_call(
        functools.partial(pack_kernel, heads),
        out_shape=[packed] * heads + [shape_of((positions.shape[1], heads * width), low)],
        in_specs=[whole_vmem] * 4 + [whole_smem] * 2,
        out_specs=[whole_vmem] * (heads + 1),
        compiler_params=params(),
        name="pack",
    )(key_rows, targets, queries, positions, retain, learn_rate)
    return outs[:heads], outs[heads]


def scan_kernel(heads, backward, with_states, *refs):
    packs, terms, start = refs[:heads], refs[heads : 2 * heads], refs[2 * heads]
    outs = refs[2 * heads + 1 : -2]
    end_ref = outs[-1]
    linear, term = refs[-2:]
    width, hidden = start.shape
    member = lax.axis_index("ctx") % heads
    for bits in range(heads):
        place = jnp.bitwise_xor(member, bits)
        linear[place] = packs[bits][:, hidden:]
        term[place] = terms[bits][:width, :hidden]
    state = start[...].astype(wide)
    order = range(heads - 1, -1, -1) if backward else range(heads)
    for place in order:
        parts = linear[place, width:, :].astype(wide)
        keep = parts[0:1, :] + parts[1:2, :] + parts[2:3, :]
        keep = jnp.concatenate([keep] * (hidden // width), axis=1)
        rounded = state.astype(low)
        added = term[place].astype(wide)
        if with_states:
            term[place] = rounded
        state = state * keep - dot(linear[place, :width, :], rounded) + added
    end_ref[...] = state.astype(low)
    if with_states:
        for bits in range(heads):
            outs[bits][...] = term[jnp.bitwise_xor(member, bits)]


def scan_call(packs, terms, start, backward, with_states):
    heads = len(packs)
    width, hidden = start.shape
    count = heads + 1 if with_states else 1
    return pl.pallas_call(
        functools.partial(scan_kernel, heads, backward, with_states),
        out_shape=[shape_of((width, hidden), low)] * count,
        in_specs=[whole_vmem] * (2 * heads + 1),
        out_specs=[whole_vmem] * count,
        scratch_shapes=[
            pltpu.VMEM((heads, width + pad_rows, width), low),
            pltpu.VMEM((heads, width, hidden), low),
        ],
        compiler_params=params(),
        name="scan_back" if backward else "scan",
    )(*packs, *terms, start)


def scanned(packs, terms, backward):
    heads = len(packs)
    width = packs[0].shape[0] - pad_rows
    hidden = packs[0].shape[1] - width
    groups = lax.axis_size("ctx") // heads
    start = jnp.zeros((width, hidden), low)
    for _ in range(groups - 1):
        end = scan_call(packs, terms, start, backward, False)[0]
        start = shifted(end, "ctx", -heads if backward else heads)
    return scan_call(packs, terms, start, backward, True)[:heads]


def read_kernel(heads, picked_ref, *refs):
    states, out = refs[:heads], refs[heads]
    width = picked_ref.shape[1] // heads
    member = lax.axis_index("ctx") % heads
    total = None
    for bits in range(heads):
        head = jnp.bitwise_xor(member, bits)
        rows = picked_ref[:, pl.ds(pl.multiple_of(head * width, width), width)]
        term = dot(rows, states[bits][...])
        total = term if total is None else total + term
    out[...] = total


def read(picked, states):
    heads = len(states)
    return pl.pallas_call(
        functools.partial(read_kernel, heads),
        out_shape=shape_of((picked.shape[0], states[0].shape[1]), wide),
        in_specs=[whole_vmem] * (heads + 1),
        out_specs=whole_vmem,
        compiler_params=params(),
        name="read",
    )(picked, *states)


def block_kernel(causal, scale, usable_ref, q_ref, k_ref, v_ref, e_ref, m_ref, l_ref, o_ref):
    scores = dot(k_ref[...], q_ref[...], 1, 1) * scale
    if causal:
        key_at = lax.broadcasted_iota(jnp.int32, scores.shape, 0)
        query_at = lax.broadcasted_iota(jnp.int32, scores.shape, 1)
        scores = jnp.where(key_at <= query_at, scores, masked)
    top = jnp.max(scores, axis=0, keepdims=True)
    weights = jnp.exp2(scores - top)
    l_ref[0] = jnp.sum(weights, axis=0, keepdims=True)
    weights = weights.astype(low)
    e_ref[0] = weights
    o_ref[0] = dot(v_ref[...], weights, 0, 0)
    m_ref[0] = jnp.where(usable_ref[0, 0] == 1, top, masked)


def block_forward(queries, pair, usable, heads, causal):
    seg_len = queries.shape[0]
    width = queries.shape[1] // heads
    scale = width**-0.5 * math.log2(math.e)
    stat = pl.BlockSpec((1, 1, seg_len), lambda h: (h, 0, 0))
    flops = 4 * heads * seg_len * seg_len * width
    return pl.pallas_call(
        functools.partial(block_kernel, causal, scale),
        grid=(heads,),
        out_shape=[
            shape_of((heads, seg_len, seg_len), low),
            shape_of((heads, 1, seg_len), wide),
            shape_of((heads, 1, seg_len), wide),
            shape_of((heads, width, seg_len), wide),
        ],
        in_specs=[
            whole_smem,
            pl.BlockSpec((seg_len, width), lambda h: (0, h)),
            pl.BlockSpec((seg_len, width), lambda h: (0, h)),
            pl.BlockSpec((seg_len, width), lambda h: (0, heads + h)),
        ],
        out_specs=[
            pl.BlockSpec((1, seg_len, seg_len), lambda h: (h, 0, 0)),
            stat,
            stat,
            pl.BlockSpec((1, width, seg_len), lambda h: (h, 0, 0)),
        ],
        compiler_params=params(1),
        cost_estimate=cost(flops, 8 * heads * seg_len * seg_len, heads * seg_len * seg_len),
        name="block_forward",
    )(usable, queries, pair, pair)


def memory_kernel(blocks, scale, hidden_ref, readout_ref, q_ref, g_ref, *refs):
    ins, outs, total_ref = refs[: 3 * blocks], refs[3 * blocks : -1], refs[-1]
    term_ref, grad_ref, dq_ref, delta_ref = outs[:4]
    factor_refs = outs[4:]
    head = pl.program_id(0)
    queries, cotangent = q_ref[...], g_ref[...]
    width = queries.shape[1]
    tokens = dot(hidden_ref[...], readout_ref[...])
    keys, values = tokens[:, :width].astype(low), tokens[:, width:].astype(low)
    scores = dot(keys, queries, 1, 1) * (scale * math.log2(math.e))
    tops = [ins[3 * b][0] for b in range(blocks)]
    top = functools.reduce(jnp.maximum, tops, jnp.max(scores, axis=0, keepdims=True))
    weights = jnp.exp2(scores - top)
    shrink = [jnp.exp2(part - top) for part in tops]
    total = jnp.sum(weights, axis=0, keepdims=True)
    for b in range(blocks):
        total = total + shrink[b] * ins[3 * b + 1][0]
    inverse = 1.0 / total
    probs = weights * inverse
    probs_low = probs.astype(low)
    factors = [part * inverse for part in shrink]
    attended = dot(values, probs_low, 0, 0)
    for b in range(blocks):
        attended = attended + ins[3 * b + 2][0] * factors[b]
        factor_refs[b][0] = factors[b]
    delta = jnp.sum(cotangent.astype(wide).T * attended, axis=0, keepdims=True)
    delta_ref[0] = delta
    grad_scores = (probs * (dot(values, cotangent, 1, 1) - delta)).astype(low)
    grad_keys = dot(grad_scores, queries) * scale
    grad_values = dot(probs_low, cotangent)
    grad = jnp.concatenate([grad_keys, grad_values], axis=1).astype(low)
    grad_ref[...] = grad
    dq_ref[0] = dot(keys, grad_scores, 0, 0)
    term = dot(grad, readout_ref[...], 1, 1)

    @pl.when(head == 0)
    def _():
        total_ref[...] = term

    @pl.when(head > 0)
    def _():
        total_ref[...] += term

    @pl.when(head == pl.num_programs(0) - 1)
    def _():
        term_ref[...] = total_ref[...]


def memory_attention(hidden_read, readout, queries, grad_out, parts, heads):
    seg_len = queries.shape[0]
    width = queries.shape[1] // heads
    tokens, hidden = hidden_read.shape
    stat = pl.BlockSpec((1, 1, seg_len), lambda h: (h, 0, 0))
    tall = pl.BlockSpec((1, width, seg_len), lambda h: (h, 0, 0))
    column = pl.BlockSpec((seg_len, width), lambda h: (0, h))
    blocks = len(parts)
    return pl.pallas_call(
        functools.partial(memory_kernel, blocks, width**-0.5),
        grid=(heads,),
        out_shape=[
            shape_of((tokens, hidden), wide),
            shape_of((tokens, 2 * heads * width), low),
            shape_of((heads, width, seg_len), wide),
        ]
        + [shape_of((heads, 1, seg_len), wide)] * (1 + blocks),
        in_specs=[
            pl.BlockSpec((tokens, hidden), lambda h: (0, 0)),
            pl.BlockSpec((hidden, 2 * width), lambda h: (0, h)),
            column,
            column,
        ]
        + [stat, stat, tall] * blocks,
        out_specs=[
            pl.BlockSpec((tokens, hidden), lambda h: (0, 0)),
            pl.BlockSpec((tokens, 2 * width), lambda h: (0, h)),
            tall,
        ]
        + [stat] * (1 + blocks),
        scratch_shapes=[pltpu.VMEM((tokens, hidden), wide)],
        compiler_params=params(1),
        cost_estimate=cost(heads * seg_len * tokens * width * 12, 8 * 1024 * 1024),
        name="memory_attention",
    )(hidden_read, readout, queries, grad_out, *[value for part in parts for value in part])


def back_kernel(blocks, merged, scale, q_ref, g_ref, delta_ref, dq_in_ref, *refs):
    ins, outs = refs[: 4 * blocks], refs[4 * blocks :]
    queries = q_ref[...]
    cotangent = g_ref[...].astype(wide).T
    grad_rows = dq_in_ref[0]
    for b in range(blocks):
        weight_ref, factor_ref, k_ref, v_ref = ins[4 * b : 4 * b + 4]
        factor = factor_ref[0]
        scaled = cotangent * factor
        scaled_rows = scaled.T.astype(low)
        weights = weight_ref[0]
        slope = dot(v_ref[...], scaled.astype(low)) - delta_ref[0] * factor
        grad_scores = (weights.astype(wide) * slope).astype(low)
        kind = outs[1 + 2 * b].dtype
        outs[1 + 2 * b][...] = (dot(grad_scores, queries) * scale).astype(kind)
        outs[2 + 2 * b][...] = dot(weights, scaled_rows).astype(kind)
        grad_rows = grad_rows + dot(k_ref[...], grad_scores, 0, 0)
    if merged:
        outs[0][...] = (grad_rows * scale).T
    else:
        outs[0][0] = grad_rows


def block_backward(queries, grad_out, delta, grad_rows, parts, heads, kind, merged):
    seg_len = queries.shape[0]
    width = queries.shape[1] // heads
    stat = pl.BlockSpec((1, 1, seg_len), lambda h: (h, 0, 0))
    tall = pl.BlockSpec((1, width, seg_len), lambda h: (h, 0, 0))
    column = pl.BlockSpec((seg_len, width), lambda h: (0, h))
    second = pl.BlockSpec((seg_len, width), lambda h: (0, heads + h))
    square = pl.BlockSpec((1, seg_len, seg_len), lambda h: (h, 0, 0))
    blocks = len(parts)
    wide_shape = shape_of((seg_len, heads * width), wide)
    return pl.pallas_call(
        functools.partial(back_kernel, blocks, merged, width**-0.5),
        grid=(heads,),
        out_shape=[wide_shape if merged else shape_of((heads, width, seg_len), wide)]
        + [shape_of((seg_len, heads * width), kind)] * (2 * blocks),
        in_specs=[column, column, stat, tall] + [square, stat, column, second] * blocks,
        out_specs=[column if merged else tall] + [column] * (2 * blocks),
        compiler_params=params(1),
        cost_estimate=cost(
            8 * blocks * heads * seg_len * seg_len * width,
            blocks * 4 * heads * seg_len * seg_len,
        ),
        name="block_backward",
    )(
        queries,
        grad_out,
        delta,
        grad_rows,
        *[value for weights, factor, pair in parts for value in (weights, factor, pair, pair)],
    )


def state_kernel(heads, picked_ref, hidden_ref, *outs):
    width = picked_ref.shape[1] // heads
    member = lax.axis_index("ctx") % heads
    grad = hidden_ref[...]
    for bits in range(heads):
        head = jnp.bitwise_xor(member, bits)
        rows = picked_ref[:, pl.ds(pl.multiple_of(head * width, width), width)]
        outs[bits][...] = dot(rows, grad, 0, 0).astype(low)


def state_grads(picked, grad_hidden, heads):
    width = picked.shape[1] // heads
    return pl.pallas_call(
        functools.partial(state_kernel, heads),
        out_shape=[shape_of((width, grad_hidden.shape[1]), low)] * heads,
        in_specs=[whole_vmem] * 2,
        out_specs=[whole_vmem] * heads,
        compiler_params=params(),
        name="state_grads",
    )(picked, grad_hidden)


def scatter_kernel(heads, place_ref, hidden_ref, rows_ref, *refs):
    states, out = refs[:heads], refs[heads]
    seg_len = rows_ref.shape[0]
    width = rows_ref.shape[1] // heads
    member = lax.axis_index("ctx") % heads
    rows = lax.broadcasted_iota(jnp.int32, (seg_len, place_ref.shape[1]), 0)
    chosen = jnp.where(rows == place_ref[...], 1.0, 0.0).astype(low)
    for bits in range(heads):
        head = jnp.bitwise_xor(member, bits)
        columns = pl.ds(pl.multiple_of(head * width, width), width)
        grad = dot(hidden_ref[...], states[bits][...], 1, 1).astype(low)
        out[:, columns] = rows_ref[:, columns] + dot(chosen, grad)


def scatter_read(positions, grad_hidden, grad_rows, states):
    heads = len(states)
    return pl.pallas_call(
        functools.partial(scatter_kernel, heads),
        out_shape=shape_of(grad_rows.shape, wide),
        in_specs=[whole_vmem] * (3 + heads),
        out_specs=whole_vmem,
        compiler_params=params(),
        cost_estimate=cost(4 * grad_rows.size * positions.shape[1], 8 * grad_rows.size),
        name="scatter_read",
    )(positions, grad_hidden, grad_rows, *states)


def final_kernel(heads, shares, key_ref, target_ref, rate_ref, total_ref, *refs):
    states, laters = refs[:heads], refs[heads : 2 * heads]
    out, pieces = refs[2 * heads], refs[2 * heads + 1 :]
    seg_len = key_ref.shape[0]
    width = key_ref.shape[1] // heads
    member = lax.axis_index("ctx") % heads
    mine = lax.axis_index("head")
    term = None
    for bits in range(heads):
        head = jnp.bitwise_xor(member, bits)
        columns = pl.ds(pl.multiple_of(head * width, width), width)
        keys, later = key_ref[:, columns], laters[bits][...]
        cross = dot(later, states[bits][...], 1, 1)
        both = (cross + cross.T) * (-rate_ref[0, head])
        grad = dot(target_ref[...], later, 1, 1) + dot(keys, both.astype(low))
        out[:, columns] = total_ref[:, columns] + grad * (1.0 / seg_len)
        part = dot(keys, later)
        term = part if term is None else term + part
    term = (term * (1.0 / seg_len)).astype(low)
    share = term.shape[1] // shares
    for bits in range(shares):
        for piece in range(shares):

            @pl.when(jnp.bitwise_xor(mine, bits) == piece)
            def _(bits=bits, piece=piece):
                pieces[bits][...] = term[:, piece * share : (piece + 1) * share]


def final_grads(key_rows, targets, learn_rate, key_total, states, laters, shares):
    heads = len(states)
    seg_len, hidden = targets.shape
    return pl.pallas_call(
        functools.partial(final_kernel, heads, shares),
        out_shape=[shape_of(key_total.shape, wide)]
        + [shape_of((seg_len, hidden // shares), low)] * shares,
        in_specs=[whole_vmem] * 2 + [whole_smem] + [whole_vmem] * (1 + 2 * heads),
        out_specs=[whole_vmem] * (1 + shares),
        compiler_params=params(),
        name="final_grads",
    )(key_rows, targets, learn_rate, key_total, *states, *laters)


def readout_kernel(hidden_ref, grad_ref, out):
    out[...] = dot(hidden_ref[...], grad_ref[...], 0, 0).astype(low)


def readout_term(hidden_read, grad_memory):
    return pl.pallas_call(
        readout_kernel,
        out_shape=shape_of((hidden_read.shape[1], grad_memory.shape[1]), low),
        in_specs=[whole_vmem] * 2,
        out_specs=whole_vmem,
        compiler_params=params(),
        name="readout_term",
    )(hidden_read, grad_memory)


def scattered(value, axis):
    count = lax.axis_size(axis)
    mine = lax.axis_index(axis)
    rows = value.shape[0] // count
    value = value.reshape(count, rows, value.shape[1])
    bits = 1
    while bits < count:
        halves = value.reshape(value.shape[0] // 2, 2, rows, value.shape[2])
        own = (mine // bits) % 2
        sent = lax.dynamic_index_in_dim(halves, 1 - own, 1, keepdims=False)
        kept = lax.dynamic_index_in_dim(halves, own, 1, keepdims=False)
        there = lax.ppermute(
            sent.astype(low), axis, [(place, place ^ bits) for place in range(count)]
        )
        value = kept.astype(wide) + there.astype(wide)
        bits *= 2
    return value.reshape(rows, value.shape[2])


def on_device(
    queries,
    key_rows,
    value_rows,
    targets,
    readout,
    retain,
    learn_rate,
    allowed,
    positions,
    grad_out,
):
    heads = retain.shape[1]
    reach = allowed.shape[1]
    shares = lax.axis_size("head")
    segment = lax.axis_index("ctx")

    packs, picked = pack(key_rows, targets, queries, positions, retain, learn_rate)
    packs = exchange(packs, "ctx")
    pair = jnp.concatenate([key_rows, value_rows], axis=1)
    pairs, usable = [pair], [jnp.ones((1, 1), jnp.int32)]
    for offset in range(1, reach + 1):
        pairs.append(shifted(pair, "ctx", offset))
        open_block = (allowed[segment, offset - 1] == 1) & (segment >= offset)
        usable.append(open_block.astype(jnp.int32).reshape(1, 1))
    blocks = [
        block_forward(queries, pairs[at], usable[at], heads, at == 0) for at in range(reach + 1)
    ]

    states = exchange(scanned(packs, packs, False), "ctx")
    hidden_read = summed(read(picked, states), "head").astype(low)

    results = memory_attention(
        hidden_read, readout, queries, grad_out, [block[1:] for block in blocks], heads
    )
    hidden_term, grad_memory, rows_memory, delta = results[:4]
    factors = results[4:]
    grad_hidden = summed(hidden_term, "head").astype(low)
    laters = exchange(state_grads(picked, grad_hidden, heads), "ctx")
    laters = exchange(scanned(packs, laters, True), "ctx")

    grads = block_backward(
        queries,
        grad_out,
        delta,
        rows_memory,
        [(blocks[at][0], factors[at], pairs[at]) for at in range(1, reach + 1)],
        heads,
        low,
        False,
    )
    own = block_backward(
        queries, grad_out, delta, grads[0], [(blocks[0][0], factors[0], pair)], heads, wide, True
    )
    key_total, value_total = own[1], own[2]
    for offset in range(1, reach + 1):
        back = jnp.concatenate(grads[2 * offset - 1 : 2 * offset + 1], axis=1)
        back = shifted(back, "ctx", -offset).astype(wide)
        key_total = key_total + back[:, : key_total.shape[1]]
        value_total = value_total + back[:, key_total.shape[1] :]
    grad_queries = scatter_read(positions, grad_hidden, own[0], states)
    grad_readout = scattered(readout_term(hidden_read, grad_memory), "ctx")

    final = final_grads(key_rows, targets, learn_rate, key_total, states, laters, shares)
    terms = exchange(final[1:], "head")
    grad_targets = functools.reduce(jnp.add, [term.astype(wide) for term in terms])
    return (grad_queries, final[0], value_total, grad_targets, grad_readout)


def solution(mesh):
    return jax.shard_map(
        on_device,
        mesh=mesh,
        in_specs=(
            P("ctx", "head"),
            P("ctx", "head"),
            P("ctx", "head"),
            P("ctx", None),
            P(None, "head"),
            P("ctx", "head"),
            P("ctx", "head"),
            P(),
            P("ctx", None),
            P("ctx", "head"),
        ),
        out_specs=(
            P("ctx", "head"),
            P("ctx", "head"),
            P("ctx", "head"),
            P("ctx", "head"),
            P("ctx", "head"),
        ),
        check_vma=False,
    )
```

```python
import functools
import math

import jax
import jax.numpy as jnp
from jax import lax
from jax.experimental import pallas as pl
from jax.experimental.pallas import tpu as pltpu
from jax.sharding import PartitionSpec as P

low = jnp.bfloat16
wide = jnp.float32
masked = -1e30
pad_rows = 16
mebi = 1024 * 1024

whole_vmem = pl.BlockSpec(memory_space=pltpu.VMEM)
whole_smem = pl.BlockSpec(memory_space=pltpu.SMEM)
whole_hbm = pl.BlockSpec(memory_space=pltpu.HBM)


def dot(left, right, left_axis=1, right_axis=0):
    return lax.dot_general(
        left, right, (((left_axis,), (right_axis,)), ((), ())), preferred_element_type=wide
    )


def shape_of(shape, dtype):
    return jax.ShapeDtypeStruct(shape, dtype)


def params(limit, grid_rank=0):
    if grid_rank == 0:
        return pltpu.CompilerParams(vmem_limit_bytes=limit * mebi)
    return pltpu.CompilerParams(
        dimension_semantics=("arbitrary",) * grid_rank, vmem_limit_bytes=limit * mebi
    )


def cost(flops, moved, exps=0):
    return pl.CostEstimate(flops=int(flops), bytes_accessed=int(moved), transcendentals=int(exps))


def exchange(pieces, axis):
    count = lax.axis_size(axis)
    return [pieces[0]] + [
        lax.ppermute(pieces[bits], axis, [(place, place ^ bits) for place in range(count)])
        for bits in range(1, len(pieces))
    ]


def shifted(value, axis, steps):
    count = lax.axis_size(axis)
    first, last = max(0, -steps), min(count, count - steps)
    return lax.ppermute(value, axis, [(place, place + steps) for place in range(first, last)])


def after(value, *others):
    return lax.optimization_barrier((value, others))[0]


def hbm(value):
    return pltpu.with_memory_space_constraint(value, pltpu.HBM)


def part_of(ref, head, heads):
    if len(ref.shape) == 3:
        return ref.at[head]
    width = ref.shape[1] // heads
    return ref.at[:, pl.ds(head * width, width)]


def stream_kernel(body, heads, scalars, held, moved, kept, sent, extra, *refs):
    def take(count):
        nonlocal refs
        first, refs = refs[:count], refs[count:]
        return list(first)

    flags, here, sources = take(scalars), take(held), take(moved)
    results, targets = take(kept), take(sent)
    slots, filled = take(moved), take(sent)
    here += take(extra)
    arrived, left = refs
    coming = [
        [
            pltpu.make_async_copy(
                part_of(source, head, heads), part_of(slot, head, heads), arrived.at[head, at]
            )
            for at, (source, slot) in enumerate(zip(sources, slots))
        ]
        for head in range(heads)
    ]
    going = [
        [
            pltpu.make_async_copy(
                part_of(slot, head, heads), part_of(target, head, heads), left.at[head, at]
            )
            for at, (slot, target) in enumerate(zip(filled, targets))
        ]
        for head in range(heads)
    ]
    for copies in coming:
        for copy in copies:
            copy.start()
    for head in range(heads):
        for copy in coming[head]:
            copy.wait()
        body(
            head,
            flags,
            here,
            [part_of(slot, head, heads) for slot in slots],
            results,
            [part_of(slot, head, heads) for slot in filled],
        )
        for copy in going[head]:
            copy.start()
    for copies in going:
        for copy in copies:
            copy.wait()


def streamed(body, name, heads, scalars, held, moved, kept, sent, flops, extra=()):
    counts = [len(part) for part in (scalars, held, moved, kept, sent, extra)]
    kernel = functools.partial(stream_kernel, body, heads, *counts)
    return pl.pallas_call(
        kernel,
        out_shape=[shape_of(*out) for out in kept] + [pltpu.HBM(*out) for out in sent],
        in_specs=[whole_smem] * len(scalars)
        + [whole_vmem] * len(held)
        + [whole_hbm] * len(moved),
        out_specs=[whole_vmem] * len(kept) + [whole_hbm] * len(sent),
        scratch_shapes=[pltpu.VMEM(part.shape, part.dtype) for part in moved]
        + [pltpu.VMEM(*out) for out in (*sent, *extra)]
        + [
            pltpu.SemaphoreType.DMA((heads, max(1, len(moved)))),
            pltpu.SemaphoreType.DMA((heads, max(1, len(sent)))),
        ],
        compiler_params=params(24),
        cost_estimate=cost(flops, mebi),
        name=name,
    )(*scalars, *held, *[hbm(part) for part in moved])


def relayed(value, far, step):
    relays = lax.axis_index("ctx") % 2 == (1 if step > 0 else 0)
    passed = jnp.where(relays, far, value)
    return exchange([value, passed], "ctx")[1], passed


def relay(reach):
    return reach == 2 and lax.axis_size("ctx") % 2 == 0


def halves_of_sum(value, axis):
    count = lax.axis_size(axis)
    there = jnp.zeros_like(value)
    bits = 1
    while bits < count:
        if bits > 1:
            value = value + there
        there = lax.ppermute(value, axis, [(place, place ^ bits) for place in range(count)])
        bits *= 2
    return value, there


def pack_kernel(
    heads, cuts, key_hbm, target_hbm, query_hbm, place_hbm, retain_hbm, rate_hbm, *rest
):
    pack_ref, picked_ref = rest[:2]
    key_ref, target_ref, query_ref, place_ref, retain_ref, rate_ref, arrived = rest[2:]
    seg_len = key_ref.shape[0]
    width = key_ref.shape[1] // heads
    hidden = target_ref.shape[1]
    step = seg_len // cuts
    copies = []
    for at, (source, target) in enumerate(
        [(key_hbm, key_ref), (target_hbm, target_ref), (query_hbm, query_ref)]
    ):
        for cut in range(cuts):
            rows = pl.ds(cut * step, step)
            copies.append(
                pltpu.make_async_copy(source.at[rows], target.at[rows], arrived.at[at * cuts + cut])
            )
    smalls = [
        pltpu.make_async_copy(source, target, arrived.at[3 * cuts + at])
        for at, (source, target) in enumerate(
            [(place_hbm, place_ref), (retain_hbm, retain_ref), (rate_hbm, rate_ref)]
        )
    ]
    for copy in smalls + copies:
        copy.start()
    for copy in smalls + copies[: 2 * cuts]:
        copy.wait()
    for head in range(heads):
        keys = key_ref[:, head * width : (head + 1) * width]
        gram = dot(keys, keys, 0, 0)
        write = dot(keys, target_ref[...], 0, 0)
        out = pack_ref.at[head]
        out[:width, :hidden] = (write * (1.0 / seg_len)).astype(low)
        out[:width, hidden:] = (gram * (rate_ref[0, head] * (1.0 / seg_len))).astype(low)
        shape = (pad_rows, hidden + width)
        value = jnp.full(shape, retain_ref[0, head], wide)
        first = value.astype(low).astype(wide)
        second = (value - first).astype(low).astype(wide)
        third = (value - first - second).astype(low).astype(wide)
        row = lax.broadcasted_iota(jnp.int32, shape, 0)
        tail = jnp.where(row == 0, first, jnp.where(row == 1, second, third))
        out[width:, :] = jnp.where(row < 3, tail, 0.0).astype(low)
    for copy in copies[2 * cuts :]:
        copy.wait()
    rows = lax.broadcasted_iota(jnp.int32, (seg_len, place_ref.shape[1]), 0)
    chosen = jnp.where(rows == place_ref[...], 1.0, 0.0).astype(low)
    picked_ref[...] = dot(chosen, query_ref[...], 0, 0).astype(low)


def pack(key_rows, targets, queries, positions, retain, learn_rate):
    heads = retain.shape[1]
    width = key_rows.shape[1] // heads
    hidden = targets.shape[1]
    cuts = 4
    outs = pl.pallas_call(
        functools.partial(pack_kernel, heads, cuts),
        out_shape=[
            shape_of((heads, width + pad_rows, hidden + width), low),
            shape_of((positions.shape[1], heads * width), low),
        ],
        in_specs=[whole_hbm] * 6,
        out_specs=[whole_vmem] * 2,
        scratch_shapes=[pltpu.VMEM(part.shape, low) for part in (key_rows, targets, queries)]
        + [pltpu.VMEM(positions.shape, jnp.int32)]
        + [pltpu.SMEM(part.shape, wide) for part in (retain, learn_rate)]
        + [pltpu.SemaphoreType.DMA((3 * cuts + 3,))],
        compiler_params=params(12),
        name="pack",
    )(
        *[
            hbm(part)
            for part in (key_rows, targets, queries, positions, retain, learn_rate)
        ]
    )
    return outs


def scan_kernel(heads, backward, with_states, pack_ref, *refs):
    terms, start, outs = refs[:heads], refs[heads], refs[heads + 1 : -1]
    end_ref, kept = outs[-1], refs[-1]
    width, hidden = start.shape
    member = lax.axis_index("ctx") % heads
    if backward:
        for bits in range(heads):
            kept[jnp.bitwise_xor(member, bits)] = terms[bits][...]
    state = start[...].astype(wide)
    order = range(heads - 1, -1, -1) if backward else range(heads)
    for place in order:
        parts = pack_ref[place, width:, hidden:].astype(wide)
        keep = parts[0:1, :] + parts[1:2, :] + parts[2:3, :]
        keep = jnp.concatenate([keep] * (hidden // width), axis=1)
        rounded = state.astype(low)
        added = kept[place] if backward else pack_ref[place, :width, :hidden]
        added = added.astype(wide)
        if with_states:
            kept[place] = rounded
        state = state * keep - dot(pack_ref[place, :width, hidden:], rounded) + added
    end_ref[...] = state.astype(low)
    if with_states:
        for bits in range(heads):
            outs[bits][...] = kept[jnp.bitwise_xor(member, bits)]


def scan_call(packs, terms, start, backward, with_states):
    heads = packs.shape[0]
    width, hidden = start.shape
    count = heads + 1 if with_states else 1
    terms = terms if backward else [start] * heads
    return pl.pallas_call(
        functools.partial(scan_kernel, heads, backward, with_states),
        out_shape=[shape_of((width, hidden), low)] * count,
        in_specs=[whole_vmem] * (heads + 2),
        out_specs=[whole_vmem] * count,
        scratch_shapes=[pltpu.VMEM((heads, width, hidden), low)],
        compiler_params=params(8),
        name="scan_back" if backward else "scan",
    )(packs, *terms, start)


def scanned(packs, terms, backward, beside):
    heads = packs.shape[0]
    width = packs.shape[1] - pad_rows
    hidden = packs.shape[2] - width
    groups = lax.axis_size("ctx") // heads
    start = jnp.zeros((width, hidden), low)
    waited = None
    for hop in range(groups - 1):
        end = scan_call(packs, terms, start, backward, False)[0]
        start = shifted(end, "ctx", -heads if backward else heads)
        if hop == 0:
            waited = beside(end)
            start = after(start, waited)
    if waited is None:
        start = after(start, beside(start))
    return scan_call(packs, terms, start, backward, True)[:heads]


def read_kernel(heads, picked_ref, *refs):
    states, out = refs[:heads], refs[heads]
    width = picked_ref.shape[1] // heads
    member = lax.axis_index("ctx") % heads
    total = None
    for bits in range(heads):
        head = jnp.bitwise_xor(member, bits)
        rows = picked_ref[:, pl.ds(pl.multiple_of(head * width, width), width)]
        term = dot(rows, states[bits][...])
        total = term if total is None else total + term
    out[...] = total


def read(picked, states):
    heads = len(states)
    return pl.pallas_call(
        functools.partial(read_kernel, heads),
        out_shape=shape_of((picked.shape[0], states[0].shape[1]), wide),
        in_specs=[whole_vmem] * (heads + 1),
        out_specs=whole_vmem,
        compiler_params=params(4),
        name="read",
    )(picked, *states)


def probabilities(keys, queries, stats, scale, mask=None):
    scores = dot(keys, queries, 1, 1) * (scale * math.log2(math.e))
    if mask is not None:
        scores = jnp.where(mask, scores, masked)
    return jnp.exp2(scores - stats[0:1]) * stats[1:2]


def causal_mask(keys, queries):
    shape = (keys.shape[0], queries.shape[0])
    key_at = lax.broadcasted_iota(jnp.int32, shape, 0)
    return key_at <= lax.broadcasted_iota(jnp.int32, shape, 1)


def block_body(causal, head, flags, held, moved, kept, sent):
    queries, keys, values = [ref[...] for ref in moved]
    scale = queries.shape[1] ** -0.5 * math.log2(math.e)
    scores = dot(keys, queries, 1, 1) * scale
    if causal:
        scores = jnp.where(causal_mask(keys, queries), scores, masked)
    top = jnp.max(scores, axis=0, keepdims=True)
    weights = jnp.exp2(scores - top)
    kept[1][head] = jnp.sum(weights, axis=0, keepdims=True)
    sent[0][...] = dot(values, weights.astype(low), 0, 0)
    kept[0][head] = jnp.where(flags[0][0, 0] == 1, top, masked)


def block_forward(queries, keys, values, usable, heads, causal):
    seg_len = queries.shape[0]
    width = queries.shape[1] // heads
    return streamed(
        functools.partial(block_body, causal),
        "block_forward",
        heads,
        [usable],
        [],
        [queries, keys, values],
        [((heads, 1, seg_len), wide)] * 2,
        [((heads, width, seg_len), wide)],
        4 * heads * seg_len * seg_len * width,
    )


def exchange_order(hidden_read):
    count, mine = lax.axis_size("ctx"), lax.axis_index("ctx")
    columns = hidden_read.shape[1]
    block = columns // count
    shape = (columns, columns)
    target = lax.broadcasted_iota(jnp.int32, shape, 1)
    place, wanted, bits = target // block, jnp.zeros(shape, jnp.int32), 1
    while bits < count:
        wanted = wanted + (place // (count // (2 * bits))) % 2 * bits
        bits *= 2
    source = jnp.bitwise_xor(wanted, mine) * block + target % block
    turn = jnp.where(lax.broadcasted_iota(jnp.int32, shape, 0) == source, 1.0, 0.0).astype(low)
    return dot(hidden_read, turn).astype(low)


def memory_body(blocks, head, flags, held, moved, kept, sent):
    ordered_ref = held[-1]
    hidden_read = (held[0][...] + held[1][...]).astype(low)
    if head == 0:
        ordered_ref[...] = exchange_order(hidden_read)
    queries, cotangent, readout = [ref[...] for ref in moved[:3]]
    width = queries.shape[1]
    scale = width**-0.5
    tokens = dot(hidden_read, readout)
    keys, values = tokens[:, :width].astype(low), tokens[:, width:].astype(low)
    scores = dot(keys, queries, 1, 1) * (scale * math.log2(math.e))
    tops = [held[2 + 2 * b][head] for b in range(blocks)]
    top = functools.reduce(jnp.maximum, tops, jnp.max(scores, axis=0, keepdims=True))
    weights = jnp.exp2(scores - top)
    shrink = [jnp.exp2(part - top) for part in tops]
    total = jnp.sum(weights, axis=0, keepdims=True)
    for b in range(blocks):
        total = total + shrink[b] * held[3 + 2 * b][head]
    inverse = 1.0 / total
    probs = weights * inverse
    probs_low = probs.astype(low)
    attended = dot(values, probs_low, 0, 0)
    for b in range(blocks):
        attended = attended + moved[3 + b][...] * (shrink[b] * inverse)
    delta = jnp.sum(cotangent.astype(wide).T * attended, axis=0, keepdims=True)
    stat_ref = kept[1]
    stat_ref[head, 0:1] = top
    stat_ref[head, 1:2] = inverse
    stat_ref[head, 2:3] = delta
    stat_ref[head, 3:4] = jnp.zeros_like(delta)
    grad_scores = (probs * (dot(values, cotangent, 1, 1) - delta)).astype(low)
    grad_keys = dot(grad_scores, queries) * scale
    grad_values = dot(probs_low, cotangent)
    grad = jnp.concatenate([grad_keys, grad_values], axis=1).astype(low)
    sent[1][...] = dot(keys, grad_scores, 0, 0)
    outer = dot(ordered_ref[...], grad, 0, 0).astype(low)
    half = outer.shape[0] // 2
    sent[0][...] = outer[:half]
    sent[2][...] = outer[half:]
    term = dot(grad, readout, 1, 1)
    kept[0][...] = term if head == 0 else kept[0][...] + term


def memory_attention(hidden_parts, readout, queries, grad_out, parts, heads):
    seg_len = queries.shape[0]
    width = queries.shape[1] // heads
    tokens, hidden = hidden_parts[0].shape
    half = ((hidden // 2, 2 * heads * width), low)
    term, stats, near, rows, far = streamed(
        functools.partial(memory_body, len(parts)),
        "memory_attention",
        heads,
        [],
        [*hidden_parts, *[value for part in parts for value in part[:2]]],
        [queries, grad_out, readout, *[part[2] for part in parts]],
        [((tokens, hidden), wide), ((heads, 4, seg_len), wide)],
        [half, ((heads, width, seg_len), wide), half],
        heads * seg_len * tokens * width * 14,
        [((tokens, hidden), low)],
    )
    return term, (near, far), rows, stats


def shown(flag, stats):
    top = jnp.where(flag[0, 0] == 1, stats[0:1], -masked)
    return jnp.concatenate([top, stats[1:3]], axis=0)


def rows_body(blocks, head, flags, held, moved, kept, sent):
    stats, grad_rows = held[0][head], moved[0][...]
    queries, cotangent = moved[1][...], moved[2][...]
    for b in range(blocks):
        keys, values = moved[3 + 2 * b][...], moved[4 + 2 * b][...]
        probs = probabilities(keys, queries, shown(flags[b], stats), queries.shape[1] ** -0.5)
        slope = dot(values, cotangent, 1, 1) - stats[2:3]
        grad_rows = grad_rows + dot(keys, (probs * slope).astype(low), 0, 0)
    sent[0][...] = grad_rows


def rows_backward(queries, grad_out, stats, grad_rows, parts, heads):
    return streamed(
        functools.partial(rows_body, len(parts)),
        "rows_backward",
        heads,
        [part[0] for part in parts],
        [stats],
        [grad_rows, queries, grad_out, *[value for part in parts for value in part[1:]]],
        [],
        [(grad_rows.shape, wide)],
        6 * len(parts) * queries.size * queries.shape[0],
    )[0]


def own_body(heads, head, flags, held, moved, kept, sent):
    stats, place_ref, hidden_ref = held[0][head], held[1], held[2]
    grad_rows, queries, cotangent, keys, values = [ref[...] for ref in moved]
    scale = queries.shape[1] ** -0.5
    probs = probabilities(keys, queries, stats, scale, causal_mask(keys, queries))
    slope = dot(values, cotangent, 1, 1) - stats[2:3]
    grad_scores = (probs * slope).astype(low)
    sent[1][...] = dot(grad_scores, queries) * scale
    sent[2][...] = dot(probs.astype(low), cotangent)
    grad_rows = ((grad_rows + dot(keys, grad_scores, 0, 0)) * scale).T
    rows = lax.broadcasted_iota(jnp.int32, (queries.shape[0], place_ref.shape[1]), 0)
    chosen = jnp.where(rows == place_ref[...], 1.0, 0.0).astype(low)
    member = lax.axis_index("ctx") % heads
    state_ref = held[3 + heads]
    if head == 0:
        for bits in range(heads):
            state_ref[jnp.bitwise_xor(member, bits)] = held[3 + bits][...]
    picked = dot(hidden_ref[...], state_ref[head], 1, 1).astype(low)
    sent[0][...] = grad_rows + dot(chosen, picked)


def own_backward(
    queries, grad_out, stats, grad_rows, keys, values, positions, grad_hidden, states
):
    heads = len(states)
    return streamed(
        functools.partial(own_body, heads),
        "own_backward",
        heads,
        [],
        [stats, positions, grad_hidden, *states],
        [grad_rows, queries, grad_out, keys, values],
        [],
        [(queries.shape, wide)] * 3,
        10 * queries.size * queries.shape[0],
        [((heads,) + states[0].shape, low)],
    )


def arrived_body(offsets, head, flags, held, moved, kept, sent):
    keys, values = moved[0][...], moved[1][...]
    scale = keys.shape[1] ** -0.5
    grad_keys, grad_values = None, moved[3][...]
    for at in range(offsets):
        stats = held[at][head]
        queries, cotangent = moved[4 + 2 * at][...], moved[5 + 2 * at][...]
        probs = probabilities(keys, queries, shown(flags[at], stats), scale)
        slope = dot(values, cotangent, 1, 1) - stats[2:3]
        term = dot((probs * slope).astype(low), queries)
        grad_keys = term if grad_keys is None else grad_keys + term
        grad_values = grad_values + dot(probs.astype(low), cotangent)
    sent[0][...] = moved[2][...] + grad_keys * scale
    sent[1][...] = grad_values


def arrived_backward(keys, values, grad_keys, grad_values, parts, heads):
    return streamed(
        functools.partial(arrived_body, len(parts)),
        "arrived_backward",
        heads,
        [part[0] for part in parts],
        [part[3] for part in parts],
        [keys, values, grad_keys, grad_values, *[value for part in parts for value in part[1:3]]],
        [],
        [(keys.shape, wide)] * 2,
        10 * len(parts) * keys.size * keys.shape[0],
    )


def state_kernel(heads, picked_ref, first_ref, second_ref, *outs):
    width = picked_ref.shape[1] // heads
    member = lax.axis_index("ctx") % heads
    grad = (first_ref[...] + second_ref[...]).astype(low)
    outs[heads][...] = grad
    for bits in range(heads):
        head = jnp.bitwise_xor(member, bits)
        rows = picked_ref[:, pl.ds(pl.multiple_of(head * width, width), width)]
        outs[bits][...] = dot(rows, grad, 0, 0).astype(low)


def state_grads(picked, grad_parts, heads):
    width = picked.shape[1] // heads
    hidden = grad_parts[0].shape[1]
    outs = pl.pallas_call(
        functools.partial(state_kernel, heads),
        out_shape=[shape_of((width, hidden), low)] * heads + [shape_of((picked.shape[0], hidden), low)],
        in_specs=[whole_vmem] * 3,
        out_specs=[whole_vmem] * (heads + 1),
        compiler_params=params(6),
        name="state_grads",
    )(picked, *grad_parts)
    return outs[:heads], outs[heads]


def share_kernel(heads, shares, key_ref, *refs):
    laters, pieces = refs[:heads], refs[heads:]
    seg_len = key_ref.shape[0]
    width = key_ref.shape[1] // heads
    member = lax.axis_index("ctx") % heads
    mine = lax.axis_index("head")
    term = None
    for bits in range(heads):
        head = jnp.bitwise_xor(member, bits)
        part = dot(key_ref[:, pl.ds(pl.multiple_of(head * width, width), width)], laters[bits][...])
        term = part if term is None else term + part
    term = (term * (1.0 / seg_len)).astype(low)
    share = term.shape[1] // shares
    for bits in range(shares):
        for piece in range(shares):

            @pl.when(jnp.bitwise_xor(mine, bits) == piece)
            def _(bits=bits, piece=piece):
                pieces[bits][...] = term[:, piece * share : (piece + 1) * share]


def target_shares(key_rows, laters, shares):
    heads = len(laters)
    seg_len, hidden = key_rows.shape[0], laters[0].shape[1]
    return pl.pallas_call(
        functools.partial(share_kernel, heads, shares),
        out_shape=[shape_of((seg_len, hidden // shares), low)] * shares,
        in_specs=[whole_vmem] * (1 + heads),
        out_specs=[whole_vmem] * shares,
        compiler_params=params(10),
        name="target_shares",
    )(key_rows, *laters)


def final_kernel(heads, key_ref, target_ref, rate_ref, total_ref, *refs):
    states, laters, out = refs[:heads], refs[heads : 2 * heads], refs[2 * heads]
    seg_len = key_ref.shape[0]
    width = key_ref.shape[1] // heads
    member = lax.axis_index("ctx") % heads
    for bits in range(heads):
        head = jnp.bitwise_xor(member, bits)
        columns = pl.ds(pl.multiple_of(head * width, width), width)
        keys, later = key_ref[:, columns], laters[bits][...]
        cross = dot(later, states[bits][...], 1, 1)
        both = (cross + cross.T) * (-rate_ref[0, head])
        grad = dot(target_ref[...], later, 1, 1) + dot(keys, both.astype(low))
        out[:, columns] = total_ref[:, columns] + grad * (1.0 / seg_len)


def final_keys(key_rows, targets, learn_rate, key_total, states, laters):
    heads = len(states)
    return pl.pallas_call(
        functools.partial(final_kernel, heads),
        out_shape=shape_of(key_total.shape, wide),
        in_specs=[whole_vmem] * 2 + [whole_smem] + [whole_vmem] * (1 + 2 * heads),
        out_specs=whole_vmem,
        compiler_params=params(14),
        cost_estimate=cost(8 * key_total.size * targets.shape[1], 6 * mebi),
        name="final_keys",
    )(key_rows, targets, learn_rate, key_total, *states, *laters)


def scattered(near, far, axis, beside):
    count, beside, bits = lax.axis_size(axis), list(beside), 1
    while True:
        if beside:
            far = after(far, beside.pop(0))
        there = lax.ppermute(
            far.astype(low), axis, [(place, place ^ bits) for place in range(count)]
        )
        value = near.astype(wide) + there.astype(wide)
        bits *= 2
        if bits == count:
            return value
        half = value.shape[0] // 2
        near, far = value[:half], value[half:]


def on_device(
    queries,
    key_rows,
    value_rows,
    targets,
    readout,
    retain,
    learn_rate,
    allowed,
    positions,
    grad_out,
):
    heads = retain.shape[1]
    reach = allowed.shape[1]
    shares = lax.axis_size("head")
    segment, count = lax.axis_index("ctx"), lax.axis_size("ctx")

    def flag(source, offset):
        row = jnp.clip(source, 0, count - 1)
        return ((allowed[row, offset - 1] == 1) & (source < count)).astype(jnp.int32).reshape(1, 1)

    offsets = range(1, reach + 1)
    relays = relay(reach)
    direct = [reach] if relays else offsets
    packs, picked = pack(key_rows, targets, queries, positions, retain, learn_rate)
    key_parts = [shifted(key_rows, "ctx", offset) for offset in direct]
    groups = [list(range(at, at + heads)) for at in range(0, count, heads)]
    packs = lax.all_to_all(packs, "ctx", 0, 0, axis_index_groups=groups)
    value_parts = [shifted(after(value_rows, packs), "ctx", offset) for offset in direct]
    usable = [
        flag(segment, offset) * (segment >= offset).astype(jnp.int32) for offset in offsets
    ]

    def forward(offset, waited):
        keys, values = key_parts[offset - 1], value_parts[offset - 1]
        return block_forward(
            after(queries, waited), keys, values, usable[offset - 1], heads, False
        )

    blocks = {}

    def beside_hop(end):
        blocks[0] = block_forward(
            after(queries, end), key_rows, value_rows, jnp.ones((1, 1), jnp.int32), heads, True
        )
        waited = [blocks[0][0]]
        if relays:
            near, _ = relayed(key_rows, after(key_parts[0], packs), 1)
            key_parts.insert(0, near)
            near_values, passed = relayed(value_rows, after(value_parts[0], end), 1)
            value_parts.insert(0, near_values)
            waited += [near, passed]
        return waited

    states = scanned(packs, packs, False, beside_hop)
    moved = states[1]
    states = exchange(states, "ctx")
    blocks[reach] = forward(reach, moved)
    partial_read = read(picked, after(states, blocks[reach][0]))
    late_queries = [shifted(after(queries, partial_read), "ctx", -offset) for offset in direct]
    hidden_parts = halves_of_sum(partial_read, "head")
    for offset in offsets[:-1]:
        blocks[offset] = forward(offset, hidden_parts[0])

    results = memory_attention(
        hidden_parts,
        readout,
        queries,
        grad_out,
        [blocks[at] for at in range(reach + 1)],
        heads,
    )
    hidden_term, outer, rows_memory, stats = results
    grad_parts = halves_of_sum(hidden_term, "head")
    late_cotangents = [
        shifted(after(grad_out, grad_parts[0]), "ctx", -offset) for offset in direct
    ]
    late_stats = [shifted(after(stats, grad_parts[0]), "ctx", -offset) for offset in offsets]
    rows_far = rows_backward(
        queries,
        grad_out,
        after(stats, grad_parts[0]),
        rows_memory,
        [(usable[at - 1], key_parts[at - 1], value_parts[at - 1]) for at in offsets],
        heads,
    )
    terms, grad_hidden = state_grads(
        picked, after(grad_parts, rows_far), heads
    )
    if relays:
        late_queries.insert(0, relayed(after(queries, grad_hidden), late_queries[0], -1)[0])
    laters = exchange(terms, "ctx")
    grad_queries, key_total, value_total = own_backward(
        queries,
        grad_out,
        stats,
        rows_far,
        key_rows,
        value_rows,
        positions,
        grad_hidden,
        states,
    )
    totals = [(key_total, value_total)]

    def add_arrived(chosen, waited):
        parts = [
            (flag(segment + at, at), late_queries[at - 1], late_cotangents[at - 1], late_stats[at - 1])
            for at in chosen
        ]
        keys = after(key_rows, waited)
        totals.append(arrived_backward(keys, value_rows, *totals[-1], parts, heads))
        return totals[-1][0]

    def beside_later_hop(end):
        if relays:
            late_cotangents.insert(0, relayed(after(grad_out, end), late_cotangents[0], -1)[0])
        done = add_arrived(offsets[-1:], end)
        return done

    laters = after(laters, (key_total, late_cotangents, late_stats))
    laters = scanned(packs, laters, True, beside_later_hop)
    moved = laters[1]
    laters = exchange(laters, "ctx")
    if len(offsets) > 1:
        add_arrived(offsets[:-1], moved)
    laters = after(laters, totals[-1][0])
    grad_readout = scattered(*outer, "ctx", [grad_parts[0], key_total, moved])
    pieces = exchange(target_shares(key_rows, laters, shares), "head")
    grad_keys = final_keys(key_rows, targets, learn_rate, totals[-1][0], states, laters)
    grad_targets = functools.reduce(jnp.add, [piece.astype(wide) for piece in pieces])
    return (grad_queries, grad_keys, totals[-1][1], grad_targets, grad_readout)


def solution(mesh):
    return jax.shard_map(
        on_device,
        mesh=mesh,
        in_specs=(
            P("ctx", "head"),
            P("ctx", "head"),
            P("ctx", "head"),
            P("ctx", None),
            P(None, "head"),
            P("ctx", "head"),
            P("ctx", "head"),
            P(),
            P("ctx", None),
            P("ctx", "head"),
        ),
        out_specs=(
            P("ctx", "head"),
            P("ctx", "head"),
            P("ctx", "head"),
            P("ctx", "head"),
            P("ctx", "head"),
        ),
        check_vma=False,
    )
```

```python
import functools
import math

import jax
import jax.numpy as jnp
from jax import lax
from jax.experimental import pallas as pl
from jax.experimental.pallas import tpu as pltpu
from jax.sharding import PartitionSpec as P

low = jnp.bfloat16
wide = jnp.float32
masked = -1e30
pad_rows = 16
mebi = 1024 * 1024

whole_vmem = pl.BlockSpec(memory_space=pltpu.VMEM)
whole_smem = pl.BlockSpec(memory_space=pltpu.SMEM)
whole_hbm = pl.BlockSpec(memory_space=pltpu.HBM)


def dot(left, right, left_axis=1, right_axis=0):
    return lax.dot_general(
        left, right, (((left_axis,), (right_axis,)), ((), ())), preferred_element_type=wide
    )


def shape_of(shape, dtype):
    return jax.ShapeDtypeStruct(shape, dtype)


def params(limit, grid_rank=0):
    if grid_rank == 0:
        return pltpu.CompilerParams(vmem_limit_bytes=limit * mebi)
    return pltpu.CompilerParams(
        dimension_semantics=("arbitrary",) * grid_rank, vmem_limit_bytes=limit * mebi
    )


def cost(flops, moved, exps=0):
    return pl.CostEstimate(flops=int(flops), bytes_accessed=int(moved), transcendentals=int(exps))


def exchange(pieces, axis):
    count = lax.axis_size(axis)
    return [pieces[0]] + [
        lax.ppermute(pieces[bits], axis, [(place, place ^ bits) for place in range(count)])
        for bits in range(1, len(pieces))
    ]


def shifted(value, axis, steps):
    count = lax.axis_size(axis)
    first, last = max(0, -steps), min(count, count - steps)
    return lax.ppermute(value, axis, [(place, place + steps) for place in range(first, last)])


def after(value, *others):
    return lax.optimization_barrier((value, others))[0]


def hbm(value):
    return pltpu.with_memory_space_constraint(value, pltpu.HBM)


def part_of(ref, head, heads):
    if len(ref.shape) == 3:
        return ref.at[head]
    width = ref.shape[1] // heads
    return ref.at[:, pl.ds(head * width, width)]


def stream_kernel(body, heads, scalars, held, moved, kept, sent, extra, *refs):
    def take(count):
        nonlocal refs
        first, refs = refs[:count], refs[count:]
        return list(first)

    flags, here, sources = take(scalars), take(held), take(moved)
    results, targets = take(kept), take(sent)
    slots, filled = take(moved), take(sent)
    here += take(extra)
    arrived, left = refs
    coming = [
        [
            pltpu.make_async_copy(
                part_of(source, head, heads), part_of(slot, head, heads), arrived.at[head, at]
            )
            for at, (source, slot) in enumerate(zip(sources, slots))
        ]
        for head in range(heads)
    ]
    going = [
        [
            pltpu.make_async_copy(
                part_of(slot, head, heads), part_of(target, head, heads), left.at[head, at]
            )
            for at, (slot, target) in enumerate(zip(filled, targets))
        ]
        for head in range(heads)
    ]
    for copies in coming:
        for copy in copies:
            copy.start()
    for head in range(heads):
        for copy in coming[head]:
            copy.wait()
        body(
            head,
            flags,
            here,
            [part_of(slot, head, heads) for slot in slots],
            results,
            [part_of(slot, head, heads) for slot in filled],
        )
        for copy in going[head]:
            copy.start()
    for copies in going:
        for copy in copies:
            copy.wait()


def streamed(body, name, heads, scalars, held, moved, kept, sent, flops, extra=()):
    counts = [len(part) for part in (scalars, held, moved, kept, sent, extra)]
    kernel = functools.partial(stream_kernel, body, heads, *counts)
    return pl.pallas_call(
        kernel,
        out_shape=[shape_of(*out) for out in kept] + [pltpu.HBM(*out) for out in sent],
        in_specs=[whole_smem] * len(scalars)
        + [whole_vmem] * len(held)
        + [whole_hbm] * len(moved),
        out_specs=[whole_vmem] * len(kept) + [whole_hbm] * len(sent),
        scratch_shapes=[pltpu.VMEM(part.shape, part.dtype) for part in moved]
        + [pltpu.VMEM(*out) for out in (*sent, *extra)]
        + [
            pltpu.SemaphoreType.DMA((heads, max(1, len(moved)))),
            pltpu.SemaphoreType.DMA((heads, max(1, len(sent)))),
        ],
        compiler_params=params(24),
        cost_estimate=cost(flops, mebi),
        name=name,
    )(*scalars, *held, *[hbm(part) for part in moved])


def relayed(value, far, step):
    relays = lax.axis_index("ctx") % 2 == (1 if step > 0 else 0)
    passed = jnp.where(relays, far, value)
    return exchange([value, passed], "ctx")[1], passed


def relay(reach):
    return reach == 2 and lax.axis_size("ctx") % 2 == 0


def halves_of_sum(value, axis):
    count = lax.axis_size(axis)
    there = jnp.zeros_like(value)
    bits = 1
    while bits < count:
        if bits > 1:
            value = value + there
        there = lax.ppermute(value, axis, [(place, place ^ bits) for place in range(count)])
        bits *= 2
    return value, there


def pack_kernel(
    heads, cuts, key_hbm, target_hbm, query_hbm, place_hbm, retain_hbm, rate_hbm, *rest
):
    pack_ref, picked_ref = rest[:2]
    key_ref, target_ref, query_ref, place_ref, retain_ref, rate_ref, arrived = rest[2:]
    seg_len = key_ref.shape[0]
    width = key_ref.shape[1] // heads
    hidden = target_ref.shape[1]
    step = seg_len // cuts
    copies = []
    for at, (source, target) in enumerate(
        [(key_hbm, key_ref), (target_hbm, target_ref), (query_hbm, query_ref)]
    ):
        for cut in range(cuts):
            rows = pl.ds(cut * step, step)
            copies.append(
                pltpu.make_async_copy(source.at[rows], target.at[rows], arrived.at[at * cuts + cut])
            )
    smalls = [
        pltpu.make_async_copy(source, target, arrived.at[3 * cuts + at])
        for at, (source, target) in enumerate(
            [(place_hbm, place_ref), (retain_hbm, retain_ref), (rate_hbm, rate_ref)]
        )
    ]
    for copy in smalls + copies:
        copy.start()
    for copy in smalls + copies[: 2 * cuts]:
        copy.wait()
    for head in range(heads):
        keys = key_ref[:, head * width : (head + 1) * width]
        gram = dot(keys, keys, 0, 0)
        write = dot(keys, target_ref[...], 0, 0)
        out = pack_ref.at[head]
        out[:width, :hidden] = (write * (1.0 / seg_len)).astype(low)
        out[:width, hidden:] = (gram * (rate_ref[0, head] * (1.0 / seg_len))).astype(low)
        shape = (pad_rows, hidden + width)
        value = jnp.full(shape, retain_ref[0, head], wide)
        first = value.astype(low).astype(wide)
        second = (value - first).astype(low).astype(wide)
        third = (value - first - second).astype(low).astype(wide)
        row = lax.broadcasted_iota(jnp.int32, shape, 0)
        tail = jnp.where(row == 0, first, jnp.where(row == 1, second, third))
        out[width:, :] = jnp.where(row < 3, tail, 0.0).astype(low)
    for copy in copies[2 * cuts :]:
        copy.wait()
    rows = lax.broadcasted_iota(jnp.int32, (seg_len, place_ref.shape[1]), 0)
    chosen = jnp.where(rows == place_ref[...], 1.0, 0.0).astype(low)
    picked_ref[...] = dot(chosen, query_ref[...], 0, 0).astype(low)


def pack(key_rows, targets, queries, positions, retain, learn_rate):
    heads = retain.shape[1]
    width = key_rows.shape[1] // heads
    hidden = targets.shape[1]
    cuts = 4
    outs = pl.pallas_call(
        functools.partial(pack_kernel, heads, cuts),
        out_shape=[
            shape_of((heads, width + pad_rows, hidden + width), low),
            shape_of((positions.shape[1], heads * width), low),
        ],
        in_specs=[whole_hbm] * 6,
        out_specs=[whole_vmem] * 2,
        scratch_shapes=[pltpu.VMEM(part.shape, low) for part in (key_rows, targets, queries)]
        + [pltpu.VMEM(positions.shape, jnp.int32)]
        + [pltpu.SMEM(part.shape, wide) for part in (retain, learn_rate)]
        + [pltpu.SemaphoreType.DMA((3 * cuts + 3,))],
        compiler_params=params(12),
        name="pack",
    )(
        *[
            hbm(part)
            for part in (key_rows, targets, queries, positions, retain, learn_rate)
        ]
    )
    return outs


def scan_kernel(heads, backward, with_states, pack_ref, *refs):
    terms, start, outs = refs[:heads], refs[heads], refs[heads + 1 : -1]
    end_ref, kept = outs[-1], refs[-1]
    width, hidden = start.shape
    member = lax.axis_index("ctx") % heads
    if backward:
        for bits in range(heads):
            kept[jnp.bitwise_xor(member, bits)] = terms[bits][...]
    state = start[...].astype(wide)
    order = range(heads - 1, -1, -1) if backward else range(heads)
    for place in order:
        parts = pack_ref[place, width:, hidden:].astype(wide)
        keep = parts[0:1, :] + parts[1:2, :] + parts[2:3, :]
        keep = jnp.concatenate([keep] * (hidden // width), axis=1)
        rounded = state.astype(low)
        added = kept[place] if backward else pack_ref[place, :width, :hidden]
        added = added.astype(wide)
        if with_states:
            kept[place] = rounded
        state = state * keep - dot(pack_ref[place, :width, hidden:], rounded) + added
    end_ref[...] = state.astype(low)
    if with_states:
        for bits in range(heads):
            outs[bits][...] = kept[jnp.bitwise_xor(member, bits)]


def scan_call(packs, terms, start, backward, with_states):
    heads = packs.shape[0]
    width, hidden = start.shape
    count = heads + 1 if with_states else 1
    terms = terms if backward else [start] * heads
    return pl.pallas_call(
        functools.partial(scan_kernel, heads, backward, with_states),
        out_shape=[shape_of((width, hidden), low)] * count,
        in_specs=[whole_vmem] * (heads + 2),
        out_specs=[whole_vmem] * count,
        scratch_shapes=[pltpu.VMEM((heads, width, hidden), low)],
        compiler_params=params(8),
        name="scan_back" if backward else "scan",
    )(packs, *terms, start)


def scanned(packs, terms, backward, beside):
    heads = packs.shape[0]
    width = packs.shape[1] - pad_rows
    hidden = packs.shape[2] - width
    groups = lax.axis_size("ctx") // heads
    start = jnp.zeros((width, hidden), low)
    waited = None
    for hop in range(groups - 1):
        end = scan_call(packs, terms, start, backward, False)[0]
        start = shifted(end, "ctx", -heads if backward else heads)
        if hop == 0:
            waited = beside(end)
            start = after(start, waited)
    if waited is None:
        start = after(start, beside(start))
    return scan_call(packs, terms, start, backward, True)[:heads]


def read_kernel(heads, picked_ref, *refs):
    states, out = refs[:heads], refs[heads]
    width = picked_ref.shape[1] // heads
    member = lax.axis_index("ctx") % heads
    total = None
    for bits in range(heads):
        head = jnp.bitwise_xor(member, bits)
        rows = picked_ref[:, pl.ds(pl.multiple_of(head * width, width), width)]
        term = dot(rows, states[bits][...])
        total = term if total is None else total + term
    out[...] = total


def read(picked, states):
    heads = len(states)
    return pl.pallas_call(
        functools.partial(read_kernel, heads),
        out_shape=shape_of((picked.shape[0], states[0].shape[1]), wide),
        in_specs=[whole_vmem] * (heads + 1),
        out_specs=whole_vmem,
        compiler_params=params(4),
        name="read",
    )(picked, *states)


def probabilities(keys, queries, stats, scale, mask=None):
    scores = dot(keys, queries, 1, 1) * (scale * math.log2(math.e))
    if mask is not None:
        scores = jnp.where(mask, scores, masked)
    return jnp.exp2(scores - stats[0:1])


def causal_mask(keys, queries):
    shape = (keys.shape[0], queries.shape[0])
    key_at = lax.broadcasted_iota(jnp.int32, shape, 0)
    return key_at <= lax.broadcasted_iota(jnp.int32, shape, 1)


def block_body(causal, head, flags, held, moved, kept, sent):
    queries, keys, values = [ref[...] for ref in moved]
    scale = queries.shape[1] ** -0.5 * math.log2(math.e)
    scores = dot(keys, queries, 1, 1) * scale
    if causal:
        scores = jnp.where(causal_mask(keys, queries), scores, masked)
    top = jnp.max(scores, axis=0, keepdims=True)
    weights = jnp.exp2(scores - top)
    kept[1][head] = jnp.sum(weights, axis=0, keepdims=True)
    sent[0][...] = dot(values, weights.astype(low), 0, 0)
    kept[0][head] = jnp.where(flags[0][0, 0] == 1, top, masked)


def block_forward(queries, keys, values, usable, heads, causal):
    seg_len = queries.shape[0]
    width = queries.shape[1] // heads
    return streamed(
        functools.partial(block_body, causal),
        "block_forward",
        heads,
        [usable],
        [],
        [queries, keys, values],
        [((heads, 1, seg_len), wide)] * 2,
        [((heads, width, seg_len), wide)],
        4 * heads * seg_len * seg_len * width,
    )


def exchange_order(hidden_read):
    count, mine = lax.axis_size("ctx"), lax.axis_index("ctx")
    columns = hidden_read.shape[1]
    block = columns // count
    shape = (columns, columns)
    target = lax.broadcasted_iota(jnp.int32, shape, 1)
    place, wanted, bits = target // block, jnp.zeros(shape, jnp.int32), 1
    while bits < count:
        wanted = wanted + (place // (count // (2 * bits))) % 2 * bits
        bits *= 2
    source = jnp.bitwise_xor(wanted, mine) * block + target % block
    turn = jnp.where(lax.broadcasted_iota(jnp.int32, shape, 0) == source, 1.0, 0.0).astype(low)
    return dot(hidden_read, turn).astype(low)


def memory_body(blocks, head, flags, held, moved, kept, sent):
    ordered_ref = held[-1]
    hidden_read = (held[0][...] + held[1][...]).astype(low)
    if head == 0:
        ordered_ref[...] = exchange_order(hidden_read)
    queries, cotangent, readout = [ref[...] for ref in moved[:3]]
    width = queries.shape[1]
    scale = width**-0.5
    tokens = dot(hidden_read, readout)
    keys, values = tokens[:, :width].astype(low), tokens[:, width:].astype(low)
    scores = dot(keys, queries, 1, 1) * (scale * math.log2(math.e))
    tops = [held[2 + 2 * b][head] for b in range(blocks)]
    top = functools.reduce(jnp.maximum, tops, jnp.max(scores, axis=0, keepdims=True))
    weights = jnp.exp2(scores - top)
    shrink = [jnp.exp2(part - top) for part in tops]
    total = jnp.sum(weights, axis=0, keepdims=True)
    for b in range(blocks):
        total = total + shrink[b] * held[3 + 2 * b][head]
    inverse = 1.0 / total
    probs = weights * inverse
    probs_low = probs.astype(low)
    attended = dot(values, probs_low, 0, 0)
    for b in range(blocks):
        attended = attended + moved[3 + b][...] * (shrink[b] * inverse)
    delta = jnp.sum(cotangent.astype(wide).T * attended, axis=0, keepdims=True)
    stat_ref = kept[1]
    stat_ref[head, 0:1] = top + jnp.log(total) * math.log2(math.e)
    stat_ref[head, 1:2] = delta
    grad_scores = (probs * (dot(values, cotangent, 1, 1) - delta)).astype(low)
    grad_keys = dot(grad_scores, queries) * scale
    grad_values = dot(probs_low, cotangent)
    grad = jnp.concatenate([grad_keys, grad_values], axis=1).astype(low)
    sent[1][...] = dot(keys, grad_scores, 0, 0)
    outer = dot(ordered_ref[...], grad, 0, 0).astype(low)
    half = outer.shape[0] // 2
    sent[0][...] = outer[:half]
    sent[2][...] = outer[half:]
    term = dot(grad, readout, 1, 1)
    kept[0][...] = term if head == 0 else kept[0][...] + term


def memory_attention(hidden_parts, readout, queries, grad_out, parts, heads):
    seg_len = queries.shape[0]
    width = queries.shape[1] // heads
    tokens, hidden = hidden_parts[0].shape
    half = ((hidden // 2, 2 * heads * width), low)
    term, stats, near, rows, far = streamed(
        functools.partial(memory_body, len(parts)),
        "memory_attention",
        heads,
        [],
        [*hidden_parts, *[value for part in parts for value in part[:2]]],
        [queries, grad_out, readout, *[part[2] for part in parts]],
        [((tokens, hidden), wide), ((heads, 2, seg_len), wide)],
        [half, ((heads, width, seg_len), wide), half],
        heads * seg_len * tokens * width * 14,
        [((tokens, hidden), low)],
    )
    return term, (near, far), rows, stats


def shown(flag, stats):
    return jnp.where(flag[0, 0] == 1, stats[0:1], -masked)


def rows_body(blocks, head, flags, held, moved, kept, sent):
    stats, grad_rows = held[0][head], moved[0][...]
    queries, cotangent = moved[1][...], moved[2][...]
    for b in range(blocks):
        keys, values = moved[3 + 2 * b][...], moved[4 + 2 * b][...]
        probs = probabilities(keys, queries, shown(flags[b], stats), queries.shape[1] ** -0.5)
        slope = dot(values, cotangent, 1, 1) - stats[1:2]
        grad_rows = grad_rows + dot(keys, (probs * slope).astype(low), 0, 0)
    sent[0][...] = grad_rows


def rows_backward(queries, grad_out, stats, grad_rows, parts, heads):
    return streamed(
        functools.partial(rows_body, len(parts)),
        "rows_backward",
        heads,
        [part[0] for part in parts],
        [stats],
        [grad_rows, queries, grad_out, *[value for part in parts for value in part[1:]]],
        [],
        [(grad_rows.shape, wide)],
        6 * len(parts) * queries.size * queries.shape[0],
    )[0]


def own_body(heads, head, flags, held, moved, kept, sent):
    stats, place_ref, hidden_ref = held[0][head], held[1], held[2]
    grad_rows, queries, cotangent, keys, values = [ref[...] for ref in moved]
    scale = queries.shape[1] ** -0.5
    probs = probabilities(keys, queries, stats, scale, causal_mask(keys, queries))
    slope = dot(values, cotangent, 1, 1) - stats[1:2]
    grad_scores = (probs * slope).astype(low)
    sent[1][...] = dot(grad_scores, queries) * scale
    sent[2][...] = dot(probs.astype(low), cotangent)
    grad_rows = ((grad_rows + dot(keys, grad_scores, 0, 0)) * scale).T
    rows = lax.broadcasted_iota(jnp.int32, (queries.shape[0], place_ref.shape[1]), 0)
    chosen = jnp.where(rows == place_ref[...], 1.0, 0.0).astype(low)
    member = lax.axis_index("ctx") % heads
    state_ref = held[3 + heads]
    if head == 0:
        for bits in range(heads):
            state_ref[jnp.bitwise_xor(member, bits)] = held[3 + bits][...]
    picked = dot(hidden_ref[...], state_ref[head], 1, 1).astype(low)
    sent[0][...] = grad_rows + dot(chosen, picked)


def own_backward(
    queries, grad_out, stats, grad_rows, keys, values, positions, grad_hidden, states
):
    heads = len(states)
    return streamed(
        functools.partial(own_body, heads),
        "own_backward",
        heads,
        [],
        [stats, positions, grad_hidden, *states],
        [grad_rows, queries, grad_out, keys, values],
        [],
        [(queries.shape, wide)] * 3,
        10 * queries.size * queries.shape[0],
        [((heads,) + states[0].shape, low)],
    )


def arrived_body(offsets, head, flags, held, moved, kept, sent):
    keys, values = moved[0][...], moved[1][...]
    scale = keys.shape[1] ** -0.5
    grad_keys, grad_values = None, moved[3][...]
    for at in range(offsets):
        stats = held[at][head]
        queries, cotangent = moved[4 + 2 * at][...], moved[5 + 2 * at][...]
        probs = probabilities(keys, queries, shown(flags[at], stats), scale)
        slope = dot(values, cotangent, 1, 1) - stats[1:2]
        term = dot((probs * slope).astype(low), queries)
        grad_keys = term if grad_keys is None else grad_keys + term
        grad_values = grad_values + dot(probs.astype(low), cotangent)
    sent[0][...] = moved[2][...] + grad_keys * scale
    sent[1][...] = grad_values


def arrived_backward(keys, values, grad_keys, grad_values, parts, heads):
    return streamed(
        functools.partial(arrived_body, len(parts)),
        "arrived_backward",
        heads,
        [part[0] for part in parts],
        [part[3] for part in parts],
        [keys, values, grad_keys, grad_values, *[value for part in parts for value in part[1:3]]],
        [],
        [(keys.shape, wide)] * 2,
        10 * len(parts) * keys.size * keys.shape[0],
    )


def state_kernel(heads, picked_ref, first_ref, second_ref, *outs):
    width = picked_ref.shape[1] // heads
    member = lax.axis_index("ctx") % heads
    grad = (first_ref[...] + second_ref[...]).astype(low)
    outs[heads][...] = grad
    for bits in range(heads):
        head = jnp.bitwise_xor(member, bits)
        rows = picked_ref[:, pl.ds(pl.multiple_of(head * width, width), width)]
        outs[bits][...] = dot(rows, grad, 0, 0).astype(low)


def state_grads(picked, grad_parts, heads):
    width = picked.shape[1] // heads
    hidden = grad_parts[0].shape[1]
    outs = pl.pallas_call(
        functools.partial(state_kernel, heads),
        out_shape=[shape_of((width, hidden), low)] * heads + [shape_of((picked.shape[0], hidden), low)],
        in_specs=[whole_vmem] * 3,
        out_specs=[whole_vmem] * (heads + 1),
        compiler_params=params(6),
        name="state_grads",
    )(picked, *grad_parts)
    return outs[:heads], outs[heads]


def share_kernel(heads, shares, key_ref, *refs):
    laters, pieces = refs[:heads], refs[heads:]
    seg_len = key_ref.shape[0]
    width = key_ref.shape[1] // heads
    member = lax.axis_index("ctx") % heads
    mine = lax.axis_index("head")
    term = None
    for bits in range(heads):
        head = jnp.bitwise_xor(member, bits)
        part = dot(key_ref[:, pl.ds(pl.multiple_of(head * width, width), width)], laters[bits][...])
        term = part if term is None else term + part
    term = (term * (1.0 / seg_len)).astype(low)
    share = term.shape[1] // shares
    for bits in range(shares):
        for piece in range(shares):

            @pl.when(jnp.bitwise_xor(mine, bits) == piece)
            def _(bits=bits, piece=piece):
                pieces[bits][...] = term[:, piece * share : (piece + 1) * share]


def target_shares(key_rows, laters, shares):
    heads = len(laters)
    seg_len, hidden = key_rows.shape[0], laters[0].shape[1]
    return pl.pallas_call(
        functools.partial(share_kernel, heads, shares),
        out_shape=[shape_of((seg_len, hidden // shares), low)] * shares,
        in_specs=[whole_vmem] * (1 + heads),
        out_specs=[whole_vmem] * shares,
        compiler_params=params(10),
        name="target_shares",
    )(key_rows, *laters)


def final_kernel(heads, key_ref, target_ref, rate_ref, total_ref, *refs):
    states, laters, out = refs[:heads], refs[heads : 2 * heads], refs[2 * heads]
    seg_len = key_ref.shape[0]
    width = key_ref.shape[1] // heads
    member = lax.axis_index("ctx") % heads
    for bits in range(heads):
        head = jnp.bitwise_xor(member, bits)
        columns = pl.ds(pl.multiple_of(head * width, width), width)
        keys, later = key_ref[:, columns], laters[bits][...]
        cross = dot(later, states[bits][...], 1, 1)
        both = (cross + cross.T) * (-rate_ref[0, head])
        grad = dot(target_ref[...], later, 1, 1) + dot(keys, both.astype(low))
        out[:, columns] = total_ref[:, columns] + grad * (1.0 / seg_len)


def final_keys(key_rows, targets, learn_rate, key_total, states, laters):
    heads = len(states)
    return pl.pallas_call(
        functools.partial(final_kernel, heads),
        out_shape=shape_of(key_total.shape, wide),
        in_specs=[whole_vmem] * 2 + [whole_smem] + [whole_vmem] * (1 + 2 * heads),
        out_specs=whole_vmem,
        compiler_params=params(14),
        cost_estimate=cost(8 * key_total.size * targets.shape[1], 6 * mebi),
        name="final_keys",
    )(key_rows, targets, learn_rate, key_total, *states, *laters)


def scattered(near, far, axis, beside):
    count, beside, bits = lax.axis_size(axis), list(beside), 1
    while True:
        if beside:
            far = after(far, beside.pop(0))
        there = lax.ppermute(
            far.astype(low), axis, [(place, place ^ bits) for place in range(count)]
        )
        value = near.astype(wide) + there.astype(wide)
        bits *= 2
        if bits == count:
            return value
        half = value.shape[0] // 2
        near, far = value[:half], value[half:]


def on_device(
    queries,
    key_rows,
    value_rows,
    targets,
    readout,
    retain,
    learn_rate,
    allowed,
    positions,
    grad_out,
):
    heads = retain.shape[1]
    reach = allowed.shape[1]
    shares = lax.axis_size("head")
    segment, count = lax.axis_index("ctx"), lax.axis_size("ctx")

    def flag(source, offset):
        row = jnp.clip(source, 0, count - 1)
        return ((allowed[row, offset - 1] == 1) & (source < count)).astype(jnp.int32).reshape(1, 1)

    offsets = range(1, reach + 1)
    relays = relay(reach)
    direct = [reach] if relays else offsets
    packs, picked = pack(key_rows, targets, queries, positions, retain, learn_rate)
    key_parts = [shifted(key_rows, "ctx", offset) for offset in direct]
    groups = [list(range(at, at + heads)) for at in range(0, count, heads)]
    packs = lax.all_to_all(packs, "ctx", 0, 0, axis_index_groups=groups)
    value_parts = [shifted(after(value_rows, packs), "ctx", offset) for offset in direct]
    usable = [
        flag(segment, offset) * (segment >= offset).astype(jnp.int32) for offset in offsets
    ]

    def forward(offset, waited):
        keys, values = key_parts[offset - 1], value_parts[offset - 1]
        return block_forward(
            after(queries, waited), keys, values, usable[offset - 1], heads, False
        )

    blocks = {}

    def beside_hop(end):
        blocks[0] = block_forward(
            after(queries, end), key_rows, value_rows, jnp.ones((1, 1), jnp.int32), heads, True
        )
        waited = [blocks[0][0]]
        if relays:
            near, _ = relayed(key_rows, after(key_parts[0], packs), 1)
            key_parts.insert(0, near)
            near_values, passed = relayed(value_rows, after(value_parts[0], end), 1)
            value_parts.insert(0, near_values)
            waited += [near, passed]
        return waited

    states = scanned(packs, packs, False, beside_hop)
    moved = states[1]
    states = exchange(states, "ctx")
    blocks[reach] = forward(reach, moved)
    partial_read = read(picked, after(states, blocks[reach][0]))
    late_queries = [shifted(after(queries, partial_read), "ctx", -offset) for offset in direct]
    hidden_parts = halves_of_sum(partial_read, "head")
    for offset in offsets[:-1]:
        blocks[offset] = forward(offset, hidden_parts[0])

    results = memory_attention(
        hidden_parts,
        readout,
        queries,
        grad_out,
        [blocks[at] for at in range(reach + 1)],
        heads,
    )
    hidden_term, outer, rows_memory, stats = results
    grad_parts = halves_of_sum(hidden_term, "head")
    late_cotangents = [
        shifted(after(grad_out, grad_parts[0]), "ctx", -offset) for offset in direct
    ]
    late_stats = [shifted(after(stats, grad_parts[0]), "ctx", -offset) for offset in offsets]
    rows_far = rows_backward(
        queries,
        grad_out,
        after(stats, (grad_parts[0], late_queries)),
        rows_memory,
        [(usable[at - 1], key_parts[at - 1], value_parts[at - 1]) for at in offsets],
        heads,
    )
    terms, grad_hidden = state_grads(
        picked, after(grad_parts, (rows_far, late_stats)), heads
    )
    if relays:
        late_queries.insert(0, relayed(after(queries, grad_hidden), late_queries[0], -1)[0])
    laters = exchange(terms, "ctx")
    grad_queries, key_total, value_total = own_backward(
        queries,
        grad_out,
        stats,
        rows_far,
        key_rows,
        value_rows,
        positions,
        grad_hidden,
        states,
    )
    totals = [(key_total, value_total)]

    def add_arrived(chosen, waited):
        parts = [
            (flag(segment + at, at), late_queries[at - 1], late_cotangents[at - 1], late_stats[at - 1])
            for at in chosen
        ]
        keys = after(key_rows, waited)
        totals.append(arrived_backward(keys, value_rows, *totals[-1], parts, heads))
        return totals[-1][0]

    def beside_later_hop(end):
        if relays:
            late_cotangents.insert(0, relayed(after(grad_out, key_total), late_cotangents[0], -1)[0])
        done = add_arrived(offsets[-1:], end)
        return done

    laters = after(laters, (key_total, late_cotangents, late_stats))
    laters = scanned(packs, laters, True, beside_later_hop)
    moved = laters[1]
    laters = exchange(laters, "ctx")
    if len(offsets) > 1:
        add_arrived(offsets[:-1], moved)
    laters = after(laters, totals[-1][0])
    grad_readout = scattered(*outer, "ctx", [grad_parts[0], key_total, moved])
    pieces = exchange(target_shares(key_rows, laters, shares), "head")
    grad_keys = final_keys(key_rows, targets, learn_rate, totals[-1][0], states, laters)
    grad_targets = functools.reduce(jnp.add, [piece.astype(wide) for piece in pieces])
    return (grad_queries, grad_keys, totals[-1][1], grad_targets, grad_readout)


def solution(mesh):
    return jax.shard_map(
        on_device,
        mesh=mesh,
        in_specs=(
            P("ctx", "head"),
            P("ctx", "head"),
            P("ctx", "head"),
            P("ctx", None),
            P(None, "head"),
            P("ctx", "head"),
            P("ctx", "head"),
            P(),
            P("ctx", None),
            P("ctx", "head"),
        ),
        out_specs=(
            P("ctx", "head"),
            P("ctx", "head"),
            P("ctx", "head"),
            P("ctx", "head"),
            P("ctx", "head"),
        ),
        check_vma=False,
    )
```

```python
import functools
import math

import jax
import jax.numpy as jnp
from jax import lax
from jax.experimental import pallas as pl
from jax.experimental.pallas import tpu as pltpu
from jax.sharding import PartitionSpec as P

low = jnp.bfloat16
wide = jnp.float32
masked = -1e30
pad_rows = 16
mebi = 1024 * 1024

whole_vmem = pl.BlockSpec(memory_space=pltpu.VMEM)
whole_smem = pl.BlockSpec(memory_space=pltpu.SMEM)
whole_hbm = pl.BlockSpec(memory_space=pltpu.HBM)


def dot(left, right, left_axis=1, right_axis=0):
    return lax.dot_general(
        left, right, (((left_axis,), (right_axis,)), ((), ())), preferred_element_type=wide
    )


def shape_of(shape, dtype):
    return jax.ShapeDtypeStruct(shape, dtype)


def params(limit, grid_rank=0):
    if grid_rank == 0:
        return pltpu.CompilerParams(vmem_limit_bytes=limit * mebi)
    return pltpu.CompilerParams(
        dimension_semantics=("arbitrary",) * grid_rank, vmem_limit_bytes=limit * mebi
    )


def cost(flops, moved, exps=0):
    return pl.CostEstimate(flops=int(flops), bytes_accessed=int(moved), transcendentals=int(exps))


def exchange(pieces, axis):
    count = lax.axis_size(axis)
    return [pieces[0]] + [
        lax.ppermute(pieces[bits], axis, [(place, place ^ bits) for place in range(count)])
        for bits in range(1, len(pieces))
    ]


def shifted(value, axis, steps):
    count = lax.axis_size(axis)
    first, last = max(0, -steps), min(count, count - steps)
    return lax.ppermute(value, axis, [(place, place + steps) for place in range(first, last)])


def after(value, *others):
    return lax.optimization_barrier((value, others))[0]


def hbm(value):
    return pltpu.with_memory_space_constraint(value, pltpu.HBM)


def part_of(ref, head, heads):
    if len(ref.shape) == 3:
        return ref.at[head]
    width = ref.shape[1] // heads
    return ref.at[:, pl.ds(head * width, width)]


def stream_kernel(body, heads, scalars, held, moved, kept, sent, extra, *refs):
    def take(count):
        nonlocal refs
        first, refs = refs[:count], refs[count:]
        return list(first)

    flags, here, sources = take(scalars), take(held), take(moved)
    results, targets = take(kept), take(sent)
    slots, filled = take(moved), take(sent)
    here += take(extra)
    arrived, left = refs
    coming = [
        [
            pltpu.make_async_copy(
                part_of(source, head, heads), part_of(slot, head, heads), arrived.at[head, at]
            )
            for at, (source, slot) in enumerate(zip(sources, slots))
        ]
        for head in range(heads)
    ]
    going = [
        [
            pltpu.make_async_copy(
                part_of(slot, head, heads), part_of(target, head, heads), left.at[head, at]
            )
            for at, (slot, target) in enumerate(zip(filled, targets))
        ]
        for head in range(heads)
    ]
    for copies in coming:
        for copy in copies:
            copy.start()
    for head in range(heads):
        for copy in coming[head]:
            copy.wait()
        body(
            head,
            flags,
            here,
            [part_of(slot, head, heads) for slot in slots],
            results,
            [part_of(slot, head, heads) for slot in filled],
        )
        for copy in going[head]:
            copy.start()
    for copies in going:
        for copy in copies:
            copy.wait()


def streamed(body, name, heads, scalars, held, moved, kept, sent, flops, extra=()):
    counts = [len(part) for part in (scalars, held, moved, kept, sent, extra)]
    kernel = functools.partial(stream_kernel, body, heads, *counts)
    return pl.pallas_call(
        kernel,
        out_shape=[shape_of(*out) for out in kept] + [pltpu.HBM(*out) for out in sent],
        in_specs=[whole_smem] * len(scalars)
        + [whole_vmem] * len(held)
        + [whole_hbm] * len(moved),
        out_specs=[whole_vmem] * len(kept) + [whole_hbm] * len(sent),
        scratch_shapes=[pltpu.VMEM(part.shape, part.dtype) for part in moved]
        + [pltpu.VMEM(*out) for out in (*sent, *extra)]
        + [
            pltpu.SemaphoreType.DMA((heads, max(1, len(moved)))),
            pltpu.SemaphoreType.DMA((heads, max(1, len(sent)))),
        ],
        compiler_params=params(24),
        cost_estimate=cost(flops, mebi),
        name=name,
    )(*scalars, *held, *[hbm(part) for part in moved])


def relayed(value, far, step):
    relays = lax.axis_index("ctx") % 2 == (1 if step > 0 else 0)
    passed = jnp.where(relays, far, value)
    return exchange([value, passed], "ctx")[1], passed


def relay(reach):
    return reach == 2 and lax.axis_size("ctx") % 2 == 0


def halves_of_sum(value, axis):
    count = lax.axis_size(axis)
    there = jnp.zeros_like(value)
    bits = 1
    while bits < count:
        if bits > 1:
            value = value + there
        there = lax.ppermute(value, axis, [(place, place ^ bits) for place in range(count)])
        bits *= 2
    return value, there


def pack_kernel(
    heads, cuts, key_hbm, target_hbm, query_hbm, place_hbm, retain_hbm, rate_hbm, *rest
):
    pack_ref, picked_ref = rest[:2]
    key_ref, target_ref, query_ref, place_ref, retain_ref, rate_ref, arrived = rest[2:]
    seg_len = key_ref.shape[0]
    width = key_ref.shape[1] // heads
    hidden = target_ref.shape[1]
    step = seg_len // cuts
    copies = []
    for at, (source, target) in enumerate(
        [(key_hbm, key_ref), (target_hbm, target_ref), (query_hbm, query_ref)]
    ):
        for cut in range(cuts):
            rows = pl.ds(cut * step, step)
            copies.append(
                pltpu.make_async_copy(source.at[rows], target.at[rows], arrived.at[at * cuts + cut])
            )
    smalls = [
        pltpu.make_async_copy(source, target, arrived.at[3 * cuts + at])
        for at, (source, target) in enumerate(
            [(place_hbm, place_ref), (retain_hbm, retain_ref), (rate_hbm, rate_ref)]
        )
    ]
    for copy in smalls + copies:
        copy.start()
    for copy in smalls + copies[: 2 * cuts]:
        copy.wait()
    for head in range(heads):
        keys = key_ref[:, head * width : (head + 1) * width]
        gram = dot(keys, keys, 0, 0)
        write = dot(keys, target_ref[...], 0, 0)
        out = pack_ref.at[head]
        out[:width, :hidden] = (write * (1.0 / seg_len)).astype(low)
        out[:width, hidden:] = (gram * (rate_ref[0, head] * (1.0 / seg_len))).astype(low)
        shape = (pad_rows, hidden + width)
        value = jnp.full(shape, retain_ref[0, head], wide)
        first = value.astype(low).astype(wide)
        second = (value - first).astype(low).astype(wide)
        third = (value - first - second).astype(low).astype(wide)
        row = lax.broadcasted_iota(jnp.int32, shape, 0)
        tail = jnp.where(row == 0, first, jnp.where(row == 1, second, third))
        out[width:, :] = jnp.where(row < 3, tail, 0.0).astype(low)
    for copy in copies[2 * cuts :]:
        copy.wait()
    rows = lax.broadcasted_iota(jnp.int32, (seg_len, place_ref.shape[1]), 0)
    chosen = jnp.where(rows == place_ref[...], 1.0, 0.0).astype(low)
    picked_ref[...] = dot(chosen, query_ref[...], 0, 0).astype(low)


def pack(key_rows, targets, queries, positions, retain, learn_rate):
    heads = retain.shape[1]
    width = key_rows.shape[1] // heads
    hidden = targets.shape[1]
    cuts = 4
    outs = pl.pallas_call(
        functools.partial(pack_kernel, heads, cuts),
        out_shape=[
            shape_of((heads, width + pad_rows, hidden + width), low),
            shape_of((positions.shape[1], heads * width), low),
        ],
        in_specs=[whole_hbm] * 6,
        out_specs=[whole_vmem] * 2,
        scratch_shapes=[pltpu.VMEM(part.shape, low) for part in (key_rows, targets, queries)]
        + [pltpu.VMEM(positions.shape, jnp.int32)]
        + [pltpu.SMEM(part.shape, wide) for part in (retain, learn_rate)]
        + [pltpu.SemaphoreType.DMA((3 * cuts + 3,))],
        compiler_params=params(12),
        name="pack",
    )(
        *[
            hbm(part)
            for part in (key_rows, targets, queries, positions, retain, learn_rate)
        ]
    )
    return outs


def scan_kernel(heads, backward, with_states, pack_ref, *refs):
    terms, start, outs = refs[:heads], refs[heads], refs[heads + 1 : -1]
    end_ref, kept = outs[-1], refs[-1]
    width, hidden = start.shape
    member = lax.axis_index("ctx") % heads
    if backward:
        for bits in range(heads):
            kept[jnp.bitwise_xor(member, bits)] = terms[bits][...]
    state = start[...].astype(wide)
    order = range(heads - 1, -1, -1) if backward else range(heads)
    for place in order:
        parts = pack_ref[place, width:, hidden:].astype(wide)
        keep = parts[0:1, :] + parts[1:2, :] + parts[2:3, :]
        keep = jnp.concatenate([keep] * (hidden // width), axis=1)
        rounded = state.astype(low)
        added = kept[place] if backward else pack_ref[place, :width, :hidden]
        added = added.astype(wide)
        if with_states:
            kept[place] = rounded
        state = state * keep - dot(pack_ref[place, :width, hidden:], rounded) + added
    end_ref[...] = state.astype(low)
    if with_states:
        for bits in range(heads):
            outs[bits][...] = kept[jnp.bitwise_xor(member, bits)]


def scan_call(packs, terms, start, backward, with_states):
    heads = packs.shape[0]
    width, hidden = start.shape
    count = heads + 1 if with_states else 1
    terms = terms if backward else [start] * heads
    return pl.pallas_call(
        functools.partial(scan_kernel, heads, backward, with_states),
        out_shape=[shape_of((width, hidden), low)] * count,
        in_specs=[whole_vmem] * (heads + 2),
        out_specs=[whole_vmem] * count,
        scratch_shapes=[pltpu.VMEM((heads, width, hidden), low)],
        compiler_params=params(8),
        name="scan_back" if backward else "scan",
    )(packs, *terms, start)


def scanned(packs, terms, backward, beside):
    heads = packs.shape[0]
    width = packs.shape[1] - pad_rows
    hidden = packs.shape[2] - width
    groups = lax.axis_size("ctx") // heads
    start = jnp.zeros((width, hidden), low)
    waited = None
    for hop in range(groups - 1):
        end = scan_call(packs, terms, start, backward, False)[0]
        start = shifted(end, "ctx", -heads if backward else heads)
        if hop == 0:
            waited = beside(end)
            start = after(start, waited)
    if waited is None:
        start = after(start, beside(start))
    return scan_call(packs, terms, start, backward, True)[:heads]


def read_kernel(heads, picked_ref, *refs):
    states, out = refs[:heads], refs[heads]
    width = picked_ref.shape[1] // heads
    member = lax.axis_index("ctx") % heads
    total = None
    for bits in range(heads):
        head = jnp.bitwise_xor(member, bits)
        rows = picked_ref[:, pl.ds(pl.multiple_of(head * width, width), width)]
        term = dot(rows, states[bits][...])
        total = term if total is None else total + term
    out[...] = total


def read(picked, states):
    heads = len(states)
    return pl.pallas_call(
        functools.partial(read_kernel, heads),
        out_shape=shape_of((picked.shape[0], states[0].shape[1]), wide),
        in_specs=[whole_vmem] * (heads + 1),
        out_specs=whole_vmem,
        compiler_params=params(4),
        name="read",
    )(picked, *states)


def probabilities(keys, queries, stats, scale, mask=None):
    scores = dot(keys, queries, 1, 1) * (scale * math.log2(math.e))
    if mask is not None:
        scores = jnp.where(mask, scores, masked)
    return jnp.exp2(scores - stats[0:1])


def causal_mask(keys, queries):
    shape = (keys.shape[0], queries.shape[0])
    key_at = lax.broadcasted_iota(jnp.int32, shape, 0)
    return key_at <= lax.broadcasted_iota(jnp.int32, shape, 1)


def block_body(causal, head, flags, held, moved, kept, sent):
    queries, keys, values = [ref[...] for ref in moved]
    scale = queries.shape[1] ** -0.5 * math.log2(math.e)
    scores = dot(keys, queries, 1, 1) * scale
    if causal:
        scores = jnp.where(causal_mask(keys, queries), scores, masked)
    top = jnp.max(scores, axis=0, keepdims=True)
    weights = jnp.exp2(scores - top)
    kept[1][head] = jnp.sum(weights, axis=0, keepdims=True)
    sent[0][...] = dot(values, weights.astype(low), 0, 0).astype(low)
    kept[0][head] = jnp.where(flags[0][0, 0] == 1, top, masked)


def block_forward(queries, keys, values, usable, heads, causal):
    seg_len = queries.shape[0]
    width = queries.shape[1] // heads
    return streamed(
        functools.partial(block_body, causal),
        "block_forward",
        heads,
        [usable],
        [],
        [queries, keys, values],
        [((heads, 1, seg_len), wide)] * 2,
        [((heads, width, seg_len), low)],
        4 * heads * seg_len * seg_len * width,
    )


def exchange_order(hidden_read):
    count, mine = lax.axis_size("ctx"), lax.axis_index("ctx")
    columns = hidden_read.shape[1]
    block = columns // count
    target = lax.broadcasted_iota(jnp.int32, (1, columns), 1)
    place, wanted, bits = target // block, jnp.zeros((1, columns), jnp.int32), 1
    while bits < count:
        wanted = wanted + (place // (count // (2 * bits))) % 2 * bits
        bits *= 2
    source = jnp.bitwise_xor(wanted, mine) * block + target % block
    rows = lax.broadcasted_iota(jnp.int32, (columns, columns), 0)
    turn = jnp.where(rows == source, 1.0, 0.0).astype(low)
    return dot(hidden_read, turn).astype(low)


def memory_body(blocks, head, flags, held, moved, kept, sent):
    ordered_ref = held[-1]
    hidden_read = (held[0][...] + held[1][...]).astype(low)
    if head == 0:
        ordered_ref[...] = exchange_order(hidden_read)
    queries, cotangent, readout = [ref[...] for ref in moved[:3]]
    width = queries.shape[1]
    scale = width**-0.5
    tokens = dot(hidden_read, readout)
    keys, values = tokens[:, :width].astype(low), tokens[:, width:].astype(low)
    scores = dot(keys, queries, 1, 1) * (scale * math.log2(math.e))
    tops = [held[2 + 2 * b][head] for b in range(blocks)]
    top = functools.reduce(jnp.maximum, tops, jnp.max(scores, axis=0, keepdims=True))
    weights = jnp.exp2(scores - top)
    shrink = [jnp.exp2(part - top) for part in tops]
    total = jnp.sum(weights, axis=0, keepdims=True)
    for b in range(blocks):
        total = total + shrink[b] * held[3 + 2 * b][head]
    inverse = 1.0 / total
    probs = weights * inverse
    probs_low = probs.astype(low)
    attended = dot(values, probs_low, 0, 0)
    for b in range(blocks):
        attended = attended + moved[3 + b][...].astype(wide) * (shrink[b] * inverse)
    delta = jnp.sum(cotangent.astype(wide).T * attended, axis=0, keepdims=True)
    stat_ref = kept[1]
    stat_ref[head, 0:1] = top + jnp.log(total) * math.log2(math.e)
    stat_ref[head, 1:2] = delta
    grad_scores = (probs * (dot(values, cotangent, 1, 1) - delta)).astype(low)
    grad_keys = dot(grad_scores, queries) * scale
    grad_values = dot(probs_low, cotangent)
    grad = jnp.concatenate([grad_keys, grad_values], axis=1).astype(low)
    sent[1][...] = dot(keys, grad_scores, 0, 0)
    outer = dot(ordered_ref[...], grad, 0, 0).astype(low)
    half = outer.shape[0] // 2
    sent[0][...] = outer[:half]
    sent[2][...] = outer[half:]
    term = dot(grad, readout, 1, 1)
    kept[0][...] = term if head == 0 else kept[0][...] + term


def memory_attention(hidden_parts, readout, queries, grad_out, parts, heads):
    seg_len = queries.shape[0]
    width = queries.shape[1] // heads
    tokens, hidden = hidden_parts[0].shape
    half = ((hidden // 2, 2 * heads * width), low)
    term, stats, near, rows, far = streamed(
        functools.partial(memory_body, len(parts)),
        "memory_attention",
        heads,
        [],
        [*hidden_parts, *[value for part in parts for value in part[:2]]],
        [queries, grad_out, readout, *[part[2] for part in parts]],
        [((tokens, hidden), wide), ((heads, 2, seg_len), wide)],
        [half, ((heads, width, seg_len), wide), half],
        heads * seg_len * tokens * width * 14,
        [((tokens, hidden), low)],
    )
    return term, (near, far), rows, stats


def shown(flag, stats):
    return jnp.where(flag[0, 0] == 1, stats[0:1], -masked)


def rows_body(blocks, head, flags, held, moved, kept, sent):
    stats, grad_rows = held[0][head], moved[0][...]
    queries, cotangent = moved[1][...], moved[2][...]
    for b in range(blocks):
        keys, values = moved[3 + 2 * b][...], moved[4 + 2 * b][...]
        probs = probabilities(keys, queries, shown(flags[b], stats), queries.shape[1] ** -0.5)
        slope = dot(values, cotangent, 1, 1) - stats[1:2]
        grad_rows = grad_rows + dot(keys, (probs * slope).astype(low), 0, 0)
    sent[0][...] = grad_rows


def rows_backward(queries, grad_out, stats, grad_rows, parts, heads):
    return streamed(
        functools.partial(rows_body, len(parts)),
        "rows_backward",
        heads,
        [part[0] for part in parts],
        [stats],
        [grad_rows, queries, grad_out, *[value for part in parts for value in part[1:]]],
        [],
        [(grad_rows.shape, wide)],
        6 * len(parts) * queries.size * queries.shape[0],
    )[0]


def own_body(heads, head, flags, held, moved, kept, sent):
    stats, place_ref, hidden_ref = held[0][head], held[1], held[2]
    grad_rows, queries, cotangent, keys, values = [ref[...] for ref in moved]
    scale = queries.shape[1] ** -0.5
    probs = probabilities(keys, queries, stats, scale, causal_mask(keys, queries))
    slope = dot(values, cotangent, 1, 1) - stats[1:2]
    grad_scores = (probs * slope).astype(low)
    sent[1][...] = dot(grad_scores, queries) * scale
    sent[2][...] = dot(probs.astype(low), cotangent)
    grad_rows = ((grad_rows + dot(keys, grad_scores, 0, 0)) * scale).T
    rows = lax.broadcasted_iota(jnp.int32, (queries.shape[0], place_ref.shape[1]), 0)
    chosen = jnp.where(rows == place_ref[...], 1.0, 0.0).astype(low)
    member = lax.axis_index("ctx") % heads
    state_ref = held[3 + heads]
    if head == 0:
        for bits in range(heads):
            state_ref[jnp.bitwise_xor(member, bits)] = held[3 + bits][...]
    picked = dot(hidden_ref[...], state_ref[head], 1, 1).astype(low)
    sent[0][...] = grad_rows + dot(chosen, picked)


def own_backward(
    queries, grad_out, stats, grad_rows, keys, values, positions, grad_hidden, states
):
    heads = len(states)
    return streamed(
        functools.partial(own_body, heads),
        "own_backward",
        heads,
        [],
        [stats, positions, grad_hidden, *states],
        [grad_rows, queries, grad_out, keys, values],
        [],
        [(queries.shape, wide)] * 3,
        10 * queries.size * queries.shape[0],
        [((heads,) + states[0].shape, low)],
    )


def arrived_body(offsets, head, flags, held, moved, kept, sent):
    keys, values = moved[0][...], moved[1][...]
    scale = keys.shape[1] ** -0.5
    grad_keys, grad_values = None, moved[3][...]
    for at in range(offsets):
        stats = held[at][head]
        queries, cotangent = moved[4 + 2 * at][...], moved[5 + 2 * at][...]
        probs = probabilities(keys, queries, shown(flags[at], stats), scale)
        slope = dot(values, cotangent, 1, 1) - stats[1:2]
        term = dot((probs * slope).astype(low), queries)
        grad_keys = term if grad_keys is None else grad_keys + term
        grad_values = grad_values + dot(probs.astype(low), cotangent)
    sent[0][...] = moved[2][...] + grad_keys * scale
    sent[1][...] = grad_values


def arrived_backward(keys, values, grad_keys, grad_values, parts, heads):
    return streamed(
        functools.partial(arrived_body, len(parts)),
        "arrived_backward",
        heads,
        [part[0] for part in parts],
        [part[3] for part in parts],
        [keys, values, grad_keys, grad_values, *[value for part in parts for value in part[1:3]]],
        [],
        [(keys.shape, wide)] * 2,
        10 * len(parts) * keys.size * keys.shape[0],
    )


def state_kernel(heads, picked_ref, first_ref, second_ref, *outs):
    width = picked_ref.shape[1] // heads
    member = lax.axis_index("ctx") % heads
    grad = (first_ref[...] + second_ref[...]).astype(low)
    outs[heads][...] = grad
    for bits in range(heads):
        head = jnp.bitwise_xor(member, bits)
        rows = picked_ref[:, pl.ds(pl.multiple_of(head * width, width), width)]
        outs[bits][...] = dot(rows, grad, 0, 0).astype(low)


def state_grads(picked, grad_parts, heads):
    width = picked.shape[1] // heads
    hidden = grad_parts[0].shape[1]
    outs = pl.pallas_call(
        functools.partial(state_kernel, heads),
        out_shape=[shape_of((width, hidden), low)] * heads + [shape_of((picked.shape[0], hidden), low)],
        in_specs=[whole_vmem] * 3,
        out_specs=[whole_vmem] * (heads + 1),
        compiler_params=params(6),
        name="state_grads",
    )(picked, *grad_parts)
    return outs[:heads], outs[heads]


def share_kernel(heads, shares, key_ref, *refs):
    laters, pieces = refs[:heads], refs[heads:]
    seg_len = key_ref.shape[0]
    width = key_ref.shape[1] // heads
    member = lax.axis_index("ctx") % heads
    mine = lax.axis_index("head")
    term = None
    for bits in range(heads):
        head = jnp.bitwise_xor(member, bits)
        part = dot(key_ref[:, pl.ds(pl.multiple_of(head * width, width), width)], laters[bits][...])
        term = part if term is None else term + part
    term = (term * (1.0 / seg_len)).astype(low)
    share = term.shape[1] // shares
    for bits in range(shares):
        for piece in range(shares):

            @pl.when(jnp.bitwise_xor(mine, bits) == piece)
            def _(bits=bits, piece=piece):
                pieces[bits][...] = term[:, piece * share : (piece + 1) * share]


def target_shares(key_rows, laters, shares):
    heads = len(laters)
    seg_len, hidden = key_rows.shape[0], laters[0].shape[1]
    return pl.pallas_call(
        functools.partial(share_kernel, heads, shares),
        out_shape=[shape_of((seg_len, hidden // shares), low)] * shares,
        in_specs=[whole_vmem] * (1 + heads),
        out_specs=[whole_vmem] * shares,
        compiler_params=params(10),
        name="target_shares",
    )(key_rows, *laters)


def final_kernel(heads, key_ref, target_ref, rate_ref, total_ref, *refs):
    states, laters, out = refs[:heads], refs[heads : 2 * heads], refs[2 * heads]
    seg_len = key_ref.shape[0]
    width = key_ref.shape[1] // heads
    member = lax.axis_index("ctx") % heads
    for bits in range(heads):
        head = jnp.bitwise_xor(member, bits)
        columns = pl.ds(pl.multiple_of(head * width, width), width)
        keys, later = key_ref[:, columns], laters[bits][...]
        cross = dot(later, states[bits][...], 1, 1)
        both = (cross + cross.T) * (-rate_ref[0, head])
        grad = dot(target_ref[...], later, 1, 1) + dot(keys, both.astype(low))
        out[:, columns] = total_ref[:, columns] + grad * (1.0 / seg_len)


def final_keys(key_rows, targets, learn_rate, key_total, states, laters):
    heads = len(states)
    return pl.pallas_call(
        functools.partial(final_kernel, heads),
        out_shape=shape_of(key_total.shape, wide),
        in_specs=[whole_vmem] * 2 + [whole_smem] + [whole_vmem] * (1 + 2 * heads),
        out_specs=whole_vmem,
        compiler_params=params(14),
        cost_estimate=cost(8 * key_total.size * targets.shape[1], 6 * mebi),
        name="final_keys",
    )(key_rows, targets, learn_rate, key_total, *states, *laters)


def scattered(near, far, axis, beside):
    count, beside, bits = lax.axis_size(axis), list(beside), 1
    while True:
        if beside:
            far = after(far, beside.pop(0))
        there = lax.ppermute(
            far.astype(low), axis, [(place, place ^ bits) for place in range(count)]
        )
        value = near.astype(wide) + there.astype(wide)
        bits *= 2
        if bits == count:
            return value
        half = value.shape[0] // 2
        near, far = value[:half], value[half:]


def on_device(
    queries,
    key_rows,
    value_rows,
    targets,
    readout,
    retain,
    learn_rate,
    allowed,
    positions,
    grad_out,
):
    heads = retain.shape[1]
    reach = allowed.shape[1]
    shares = lax.axis_size("head")
    segment, count = lax.axis_index("ctx"), lax.axis_size("ctx")

    def flag(source, offset):
        row = jnp.clip(source, 0, count - 1)
        return ((allowed[row, offset - 1] == 1) & (source < count)).astype(jnp.int32).reshape(1, 1)

    offsets = range(1, reach + 1)
    relays = relay(reach)
    direct = [reach] if relays else offsets
    packs, picked = pack(key_rows, targets, queries, positions, retain, learn_rate)
    key_parts = [shifted(key_rows, "ctx", offset) for offset in direct]
    groups = [list(range(at, at + heads)) for at in range(0, count, heads)]
    packs = lax.all_to_all(packs, "ctx", 0, 0, axis_index_groups=groups)
    value_parts = [shifted(after(value_rows, packs), "ctx", offset) for offset in direct]
    usable = [
        flag(segment, offset) * (segment >= offset).astype(jnp.int32) for offset in offsets
    ]

    def forward(offset, waited):
        keys, values = key_parts[offset - 1], value_parts[offset - 1]
        return block_forward(
            after(queries, waited), keys, values, usable[offset - 1], heads, False
        )

    blocks = {}

    def beside_hop(end):
        blocks[0] = block_forward(
            after(queries, end), key_rows, value_rows, jnp.ones((1, 1), jnp.int32), heads, True
        )
        waited = [blocks[0][0]]
        if relays:
            near, _ = relayed(key_rows, after(key_parts[0], packs), 1)
            key_parts.insert(0, near)
            near_values, passed = relayed(value_rows, after(value_parts[0], end), 1)
            value_parts.insert(0, near_values)
            waited += [near, passed]
        return waited

    states = scanned(packs, packs, False, beside_hop)
    moved = states[1]
    states = exchange(states, "ctx")
    blocks[reach] = forward(reach, moved)
    partial_read = read(picked, after(states, blocks[reach][0]))
    late_queries = [shifted(after(queries, partial_read), "ctx", -offset) for offset in direct]
    hidden_parts = halves_of_sum(partial_read, "head")
    for offset in offsets[:-1]:
        blocks[offset] = forward(offset, hidden_parts[0])

    results = memory_attention(
        hidden_parts,
        readout,
        queries,
        grad_out,
        [blocks[at] for at in range(reach + 1)],
        heads,
    )
    hidden_term, outer, rows_memory, stats = results
    grad_parts = halves_of_sum(hidden_term, "head")
    late_cotangents = [
        shifted(after(grad_out, grad_parts[0]), "ctx", -offset) for offset in direct
    ]
    late_stats = [shifted(after(stats, grad_parts[0]), "ctx", -offset) for offset in offsets]
    rows_far = rows_backward(
        queries,
        grad_out,
        after(stats, (grad_parts[0], late_queries)),
        rows_memory,
        [(usable[at - 1], key_parts[at - 1], value_parts[at - 1]) for at in offsets],
        heads,
    )
    terms, grad_hidden = state_grads(
        picked, after(grad_parts, (rows_far, late_stats)), heads
    )
    if relays:
        late_queries.insert(0, relayed(after(queries, grad_hidden), late_queries[0], -1)[0])
    laters = exchange(terms, "ctx")
    grad_queries, key_total, value_total = own_backward(
        queries,
        grad_out,
        stats,
        rows_far,
        key_rows,
        value_rows,
        positions,
        grad_hidden,
        states,
    )
    totals = [(key_total, value_total)]

    def add_arrived(chosen, waited):
        parts = [
            (flag(segment + at, at), late_queries[at - 1], late_cotangents[at - 1], late_stats[at - 1])
            for at in chosen
        ]
        keys = after(key_rows, waited)
        totals.append(arrived_backward(keys, value_rows, *totals[-1], parts, heads))
        return totals[-1][0]

    def beside_later_hop(end):
        if relays:
            late_cotangents.insert(0, relayed(after(grad_out, key_total), late_cotangents[0], -1)[0])
        done = add_arrived(offsets[-1:], end)
        return done

    laters = after(laters, (key_total, late_cotangents, late_stats))
    laters = scanned(packs, laters, True, beside_later_hop)
    moved = laters[1]
    laters = exchange(laters, "ctx")
    if len(offsets) > 1:
        add_arrived(offsets[:-1], moved)
    laters = after(laters, totals[-1][0])
    grad_readout = scattered(*outer, "ctx", [grad_parts[0], key_total, moved])
    pieces = exchange(target_shares(key_rows, laters, shares), "head")
    grad_keys = final_keys(key_rows, targets, learn_rate, totals[-1][0], states, laters)
    grad_targets = functools.reduce(jnp.add, [piece.astype(wide) for piece in pieces])
    return (grad_queries, grad_keys, totals[-1][1], grad_targets, grad_readout)


def solution(mesh):
    return jax.shard_map(
        on_device,
        mesh=mesh,
        in_specs=(
            P("ctx", "head"),
            P("ctx", "head"),
            P("ctx", "head"),
            P("ctx", None),
            P(None, "head"),
            P("ctx", "head"),
            P("ctx", "head"),
            P(),
            P("ctx", None),
            P("ctx", "head"),
        ),
        out_specs=(
            P("ctx", "head"),
            P("ctx", "head"),
            P("ctx", "head"),
            P("ctx", "head"),
            P("ctx", "head"),
        ),
        check_vma=False,
    )
```
